256 devices in a mesh: blk: 4 (over y), branch: 64 (over z, x, core).
Axes of the slice: x: 4, y: 4, z: 8, core: 2. Of those that a mesh axis runs over, the one named last changes fastest.
Arguments:
- queries: bfloat16 [128, 32, 8192], P('branch', None, 'blk'), may hold values from -400 to 400
- root_kv: bfloat16 [4096, 2, 1024], P('branch', None, 'blk'), may hold values from -6 to 6
- node_kv: bfloat16 [192, 128, 2, 1024], P('branch', None, None, 'blk'), may hold values from -6 to 6
- own_kv: bfloat16 [128, 32, 2, 1024], P('branch', None, None, 'blk'), may hold values from -6 to 6
- anc_owner: int32 [128, 8], P('branch'), may hold values from 0 to 63, all different within a row; in each aligned block of 2 rows (0 to 1, 2 to 3, ...) at most 2 rows name the same one
- anc_slot: int32 [128, 8], P('branch'), may hold values from 0 to 2
- depth_len: int32 [128], P('branch'), may hold values from 1 to 8
- seg_len: int32 [128], P('branch'), may hold values from 1 to 32
- norm_gain: bfloat16 [8192], P('blk'), may hold values from 0.099609375 to 1.8984375
Outputs:
- normed: bfloat16 [128, 32, 8192], P('branch', None, 'blk')
The draws below stay inside these ranges and needn't reach their ends.
Inputs may be any that keep to these rules, and one draw needn't show every extreme that they name: `anc_owner`: each branch's row names 8 different owners; among the 2 rows of one index of branch, no owner is named more than 2 times, a bound that some block reaches.
All inputs are finite; a program needn't handle non-finite values.
Results may differ from the reference program's by a relative error of at most 0.008.
Values may be sent and summed in bfloat16 or wider, within the bound.
A program may use at most 128 MiB of HBM per device.

```python
import math
import jax
import jax.numpy as jnp
import numpy as np
from jax import lax

HEADS = 64
KV_HEADS = 8
HEAD_DIM = 128
BLK = 128
DEPTH = 8
SEG = 32
BR_DEV = 2
NODE_DEV = 3
BRANCHES = 128
NODES = 192
CTX = 4096
CAP = 2
N_BRANCH = 64


def draw_queries(key, part):
    key = jax.random.fold_in(key, 11)
    base = jnp.clip(jax.random.normal(key, (BRANCHES, SEG, HEADS * HEAD_DIM), jnp.float32), -6.0, 6.0)
    return base.astype(jnp.bfloat16)


def plant(array, stream_key, smallest, high):
    extent = array.shape
    place = [jax.random.randint(jax.random.fold_in(stream_key, axis), (), 0, extent[axis]) for axis in range(len(extent))]
    array = array.at[tuple(place)].set(smallest)
    longest = extent.index(max(extent))
    place[longest] = (place[longest] + 1) % extent[longest]
    return array.at[tuple(place)].set(high)


def block_scale(key, dims, shards, low, high):
    def one(axis_at, blocks):
        steps = jax.random.uniform(jax.random.fold_in(jax.random.fold_in(key, 6), axis_at), (blocks,), jnp.float32, low / len(shards), high / len(shards))
        return jnp.repeat(jnp.exp(steps), dims[axis_at] // blocks).reshape((-1,) + (1,) * (len(dims) - axis_at - 1))

    factor_of = one(*shards[0])
    for cut in shards[1:]:
        factor_of = factor_of * one(*cut)
    return factor_of


def deal_out(key, own, number, rows, amount, top, bound, slope):
    ranking = jax.random.permutation(key, amount)
    crowded, common = shares(amount, rows * top, bound, slope, True), shares(amount, rows * top, bound, slope, False)
    places = jnp.arange(amount)

    def named(sizes, rotation):
        used = int((sizes > 0).sum())
        fixed = max(1, used // 4)
        passed = fixed + (places - fixed + rotation * (used - fixed)) % max(1, amount - fixed)
        return jnp.zeros((amount,), jnp.int32).at[ranking[jnp.where(places < fixed, places, passed)]].set(jnp.asarray(sizes, jnp.int32))

    sizes = jnp.where(number % 4 == 0, named(crowded, number // 4), named(common, number - number // 4 - 1))
    mixed = jax.random.permutation(jax.random.fold_in(own, 3), amount)
    source_of, taker = mixed[0:amount // 2 * 2:2], mixed[1:amount // 2 * 2:2]
    slack = jnp.minimum(sizes[source_of] - 1, bound - sizes[taker]) // 2
    slack = jnp.where((source_of == ranking[0]) | (taker == ranking[0]) | (sizes[taker] == 0), 0, jnp.maximum(slack, 0))
    passed = jax.random.randint(jax.random.fold_in(own, 4), (amount // 2,), 0, 1 << 20) % (slack + 1)
    sizes = sizes.at[source_of].add(-passed).at[taker].add(passed)
    labels = jnp.searchsorted(jnp.cumsum(sizes), jnp.arange(rows * top), side="right").astype(jnp.int32)
    grid = labels.reshape(top, rows).T
    grid = grid[jax.random.permutation(jax.random.fold_in(own, 1), rows)]
    rotation = jax.random.randint(jax.random.fold_in(own, 2), (rows, 1), 0, top)
    return jnp.take_along_axis(grid, (jnp.arange(top)[None, :] + rotation) % top, axis=1)


def shares(count, total, most, skew, full):
    weights = [(1 << 20) // math.isqrt(grade ** skew) + 1 for grade in range(1, count + 1)]
    largest = most if full else min(most, max(-(-total // count), total * weights[0] // sum(weights)))
    least = 1 if total - largest >= count - 1 else 0
    holding, rest = [largest] + [least] * (count - 1), total - largest - least * (count - 1)
    while rest > 0:
        candidates = [i for i in range(1, count) if holding[i] < largest] or [i for i in range(1, count) if holding[i] < most]
        mass, left = sum([weights[i] for i in candidates]), rest
        for i in candidates:
            addition = min(most - holding[i], max(1, left * weights[i] // mass), rest)
            holding[i] = holding[i] + addition
            rest = rest - addition
    return np.array(holding)


def centred(own_key, shape, scale, reach, shards=(), dtype=jnp.bfloat16):
    level = block_scale(own_key, shape, shards, -0.22, 0.18) if shards else 1.0
    values = jax.random.normal(own_key, shape, jnp.float32) * scale * level
    return jnp.minimum(jnp.maximum(values, -reach), reach).astype(dtype)


def setup_inputs(seed: int = 0) -> dict:
    arg_keys = jax.random.split(jax.random.key(seed), 10)
    queries = draw_queries(jax.random.fold_in(arg_keys[9], 71), 0)
    root_kv = centred(arg_keys[1], (CTX, 2, KV_HEADS * HEAD_DIM), 1.0, 6.0, ((0, 64), (2, 4)))
    node_kv = centred(arg_keys[2], (NODES, BLK, 2, KV_HEADS * HEAD_DIM), 1.0, 6.0, ((0, 64), (3, 4)))
    own_kv = centred(arg_keys[3], (BRANCHES, SEG, 2, KV_HEADS * HEAD_DIM), 1.0, 6.0, ((0, 64), (3, 4)))
    anc_owner_keys = jax.random.split(jax.random.fold_in(arg_keys[4], 1), BRANCHES // BR_DEV)
    anc_owner_turns = jax.random.permutation(jax.random.fold_in(arg_keys[4], 3), BRANCHES // BR_DEV)
    anc_owner = jax.vmap(lambda own, number: deal_out(jax.random.fold_in(arg_keys[4], 2), own, number, BR_DEV, N_BRANCH, DEPTH, CAP, 2))(anc_owner_keys, anc_owner_turns).reshape((BRANCHES, DEPTH))
    anc_slot = plant(jax.random.randint(arg_keys[5], (BRANCHES, DEPTH), 0, NODE_DEV), jax.random.fold_in(arg_keys[5], 1), 0, NODE_DEV - 1).astype(jnp.int32)
    depth_len = plant(jax.random.randint(arg_keys[6], (BRANCHES,), 1, DEPTH + 1), jax.random.fold_in(arg_keys[6], 1), 1, DEPTH).astype(jnp.int32)
    seg_len = plant(jax.random.randint(arg_keys[7], (BRANCHES,), 1, SEG + 1), jax.random.fold_in(arg_keys[7], 1), 1, SEG).astype(jnp.int32)
    norm_gain = jnp.clip(1.0 + 0.18 * jax.random.normal(arg_keys[8], (HEADS * HEAD_DIM,), jnp.float32), 0.099609375, 1.8984375).astype(jnp.bfloat16)
    return {"queries": queries, "root_kv": root_kv, "node_kv": node_kv, "own_kv": own_kv, "anc_owner": anc_owner, "anc_slot": anc_slot, "depth_len": depth_len, "seg_len": seg_len, "norm_gain": norm_gain}


def reference(queries, root_kv, node_kv, own_kv, anc_owner, anc_slot, depth_len, seg_len, norm_gain):
    group = HEADS // KV_HEADS
    scale = 1.0 / math.sqrt(HEAD_DIM)
    root_keys = root_kv[:, 0].reshape(CTX, KV_HEADS, HEAD_DIM)
    root_values = root_kv[:, 1].reshape(CTX, KV_HEADS, HEAD_DIM)
    nodes = (anc_owner * NODE_DEV + anc_slot).astype(jnp.int32)
    positions = jnp.arange(SEG)
    levels_of = jnp.arange(DEPTH * BLK) // BLK

    def one_branch(packed):
        query, node_ids, levels, length, own = packed
        heads = query.reshape(SEG, KV_HEADS, group, HEAD_DIM).astype(jnp.float32)
        blocks = node_kv[node_ids]
        tree_keys = blocks[:, :, 0].reshape(DEPTH * BLK, KV_HEADS, HEAD_DIM)
        tree_values = blocks[:, :, 1].reshape(DEPTH * BLK, KV_HEADS, HEAD_DIM)
        own_keys = own[:, 0].reshape(SEG, KV_HEADS, HEAD_DIM)
        own_values = own[:, 1].reshape(SEG, KV_HEADS, HEAD_DIM)
        keys = jnp.concatenate([root_keys, tree_keys, own_keys], axis=0).astype(jnp.float32)
        values = jnp.concatenate([root_values, tree_values, own_values], axis=0).astype(jnp.float32)
        seen_root = jnp.ones((SEG, CTX), bool)
        seen_tree = jnp.broadcast_to((levels_of < levels)[None, :], (SEG, DEPTH * BLK))
        seen_own = positions[None, :] <= positions[:, None]
        seen = jnp.concatenate([seen_root, seen_tree, seen_own], axis=1)[:, None, None, :]
        scores = jnp.einsum('skgd,nkd->skgn', heads, keys) * scale
        scores = jnp.where(seen, scores, -1e+30)
        top = lax.optimization_barrier(jnp.max(scores, axis=-1, keepdims=True))
        weights = jnp.where(seen, jnp.exp(scores - top), 0.0)
        total = lax.optimization_barrier(jnp.sum(weights, axis=-1))
        rounded = lax.optimization_barrier(weights.astype(jnp.bfloat16)).astype(jnp.float32)
        attended = jnp.einsum('skgn,nkd->skgd', rounded, values) / total[..., None]
        attended = attended.reshape(SEG, HEADS * HEAD_DIM)
        attended = jnp.where((positions < length)[:, None], attended, 0.0)
        mean_square = lax.optimization_barrier(jnp.sum(attended * attended, axis=-1)) / (HEADS * HEAD_DIM) + 1e-06
        result = attended * lax.rsqrt(mean_square)[:, None] * norm_gain.astype(jnp.float32)[None, :]
        return result.astype(jnp.bfloat16)
    return lax.map(one_branch, (queries, nodes, depth_len, seg_len, own_kv))
```

```python
import functools
import math

import jax
import jax.numpy as jnp
from jax import lax
from jax.experimental import pallas as pl
from jax.experimental.pallas import tpu as pltpu
from jax.sharding import PartitionSpec as P

MESH = pl.DeviceIdType.MESH
HEADS = 64
DIM = 128
SEG = 32
GROUP = 8
SLOTS = 3
ROWS = GROUP * SEG
ROOT = 64
ZN = 8
XN = 4
C2 = math.log2(math.e) / math.sqrt(DIM)
NEG = -1e30
TAIL = 16
POS_DZ = (0, -1, 1, -2, 2, -3, 3, 4)
STAGES = ((0, 1, 2), (3, 4), (5, 6), (7,))
NPIECE = 6


def pos_of(step, direction):
    return 7 if step == 4 else 2 * step - 1 + direction


def kernel(
    q_hbm, root_x, node_x, own_x, owner_s, slot_s, depth_s, seg_s, gain_ref, out_ref,
    qbuf, rk, rv, rvt, ownk, ownv,
    n000, n001, n002, n003, n010, n011, n012, n013,
    n100, n101, n102, n103, n110, n111, n112, n113,
    acc, md, s0, s1, r0, r1, tbuf, tsm, sendbuf, recvbuf, att, ssq, ssq_in,
    zsend, zrecv, csend, crecv, qsend, qrecv, tsend, trecv, osend, orecv, ysend, yrecv, lsem,
):
    bf16, f32 = jnp.bfloat16, jnp.float32
    nodes = (
        ((n000, n001, n002, n003), (n010, n011, n012, n013)),
        ((n100, n101, n102, n103), (n110, n111, n112, n113)),
    )
    y = lax.axis_index("blk")
    r = lax.axis_index("branch")
    z, x, c = r // 8, (r // 2) % 4, r % 2

    def dev(dy=0, dz=0, dx=0, dc=0):
        zz = lax.rem(z + dz + ZN, ZN)
        xx = lax.rem(x + dx + XN, XN)
        cc = lax.rem(c + dc, 2)
        return (lax.rem(y + dy, 4), zz * 8 + xx * 2 + cc)

    bar = pltpu.get_barrier_semaphore()
    peers = [dev(dz=1), dev(dz=-1), dev(dc=1)]
    peers += [dev(dx=d) for d in (1, 2, 3)] + [dev(dy=d) for d in (1, 2, 3)]
    for p in peers:
        pl.semaphore_signal(bar, inc=1, device_id=p, device_id_type=MESH)

    qcopy = pltpu.make_async_copy(q_hbm, qbuf.at[3], lsem.at[0])
    qcopy.start()

    row = lax.broadcasted_iota(jnp.int32, (128, 128), 0)
    col = lax.broadcasted_iota(jnp.int32, (128, 128), 1)
    want = (row % 32) * 4 + row // 32
    pick = jnp.where(col == want, 1.0, 0.0).astype(bf16)

    def apart(ref, first):
        return jnp.dot(pick, ref[first : first + 128, :], preferred_element_type=f32)

    for t in range(2):
        got = apart(root_x, t * 128).astype(bf16)
        for h in range(2):
            rk[0, 0, h, t * 32 : t * 32 + 32, :] = got[h * 64 : h * 64 + 32]
            rv[0, 0, h, t * 32 : t * 32 + 32, :] = got[h * 64 + 32 : h * 64 + 64]
    for s in range(SLOTS):
        got = [apart(node_x, (s * 4 + t) * 128) for t in range(4)]
        for h in range(2):
            keys = jnp.concatenate([g[h * 64 : h * 64 + 32] for g in got], axis=0)
            vals = jnp.concatenate([g[h * 64 + 32 : h * 64 + 64] for g in got], axis=0)
            nodes[h][0][0][0, 0, s] = keys.astype(bf16)
            nodes[h][1][0][0, 0, s] = jnp.transpose(vals).astype(bf16)
    zeros96 = jnp.zeros((96, 128), f32)
    for b in range(2):
        got = apart(own_x, b * 128)
        for h in range(2):
            keys = jnp.concatenate([got[h * 64 : h * 64 + 32], zeros96], axis=0)
            vals = jnp.concatenate([got[h * 64 + 32 : h * 64 + 64], zeros96], axis=0)
            ownk[b, h] = keys.astype(bf16)
            ownv[b, h] = jnp.transpose(vals).astype(bf16)
    lane = lax.broadcasted_iota(jnp.int32, (8, 128), 1)
    sub = lax.broadcasted_iota(jnp.int32, (8, 128), 0)
    table = jnp.zeros((8, 128), jnp.int32)
    for b in range(2):
        for l in range(8):
            name = jnp.where(l < depth_s[b], owner_s[b, l], -1)
            table = jnp.where((lane == name) & (sub == b), slot_s[b, l] + 1, table)
    tbuf[3] = table

    pl.semaphore_wait(bar, len(peers))

    def view(piece, pos, core):
        if piece < 2:
            return (rk, rv)[piece].at[pos, core]
        for st, members in enumerate(STAGES):
            if pos in members:
                return nodes[piece // 2 - 1][piece % 2][st].at[members.index(pos), core]

    started = []

    def zcopy(piece, direction, step):
        src = view(piece, 0 if step == 1 else pos_of(step - 1, direction), 0)
        dst = view(piece, pos_of(step, direction), 0)
        return pltpu.make_async_remote_copy(
            src, dst, zsend.at[piece, direction, step - 1], zrecv.at[piece, direction, step - 1],
            device_id=dev(dz=1 if direction == 0 else -1), device_id_type=MESH,
        )

    def ccopy(piece, pos):
        return pltpu.make_async_remote_copy(
            view(piece, pos, 0), view(piece, pos, 1), csend.at[piece, pos], crecv.at[piece, pos],
            device_id=dev(dc=1), device_id_type=MESH,
        )

    def go(copy):
        copy.start()
        started.append(copy)

    def exists(piece, direction, step):
        return step <= 3 or (step == 4 and piece % 2 == direction)

    def begin(piece):
        for direction in (0, 1):
            go(zcopy(piece, direction, 1))
        go(ccopy(piece, 0))

    def forward(piece, step):
        for direction in (0, 1):
            if exists(piece, direction, step):
                zcopy(piece, direction, step).wait_recv()
                if exists(piece, direction, step + 1):
                    go(zcopy(piece, direction, step + 1))
                go(ccopy(piece, pos_of(step, direction)))

    def settle(piece, stage):
        for pos in STAGES[stage]:
            ccopy(piece, pos).wait_recv()

    def xcopies(j):
        to = dev(dx=j + 1)
        qc = pltpu.make_async_remote_copy(
            qbuf.at[3], qbuf.at[2 - j], qsend.at[j], qrecv.at[2 - j], device_id=to, device_id_type=MESH
        )
        tc = pltpu.make_async_remote_copy(
            tbuf.at[3], tbuf.at[2 - j], tsend.at[j], trecv.at[2 - j], device_id=to, device_id_type=MESH
        )
        return qc, tc

    begin(0)
    begin(1)
    for j in range(3):
        go(xcopies(j)[1])
    qcopy.wait()
    for j in (0, 2, 1):
        go(xcopies(j)[0])
    begin(2)
    begin(3)

    def queries_of(u, h):
        j, b = u // 2, u % 2
        parts = [qbuf[j, b, :, h * 1024 + g * 128 : h * 1024 + g * 128 + 128] for g in range(GROUP)]
        return jnp.concatenate(parts, axis=0)

    def scores_of(keys, q):
        return lax.dot_general(keys, q, (((1,), (1,)), ((), ())), preferred_element_type=f32)

    def with_ones(vt):
        return jnp.concatenate([vt, jnp.ones((TAIL, vt.shape[1]), bf16)], axis=0)

    def clear(u, _):
        for h in range(2):
            acc[u, h] = jnp.zeros((DIM + TAIL, ROWS), f32)
            md[u, h] = jnp.full((8, ROWS), NEG, f32)
        return 0

    lax.fori_loop(0, 6, clear, 0)
    key_at = lax.broadcasted_iota(jnp.int32, (128, ROWS), 0)
    query_at = lax.rem(lax.broadcasted_iota(jnp.int32, (128, ROWS), 1), SEG)
    causal = key_at <= query_at
    for b in range(2):
        for h in range(2):
            s = scores_of(ownk[b, h], queries_of(6 + b, h))
            s = jnp.where(causal, s, NEG)
            m = jnp.max(s, axis=0, keepdims=True)
            p = jnp.exp2(s * C2 - m * C2).astype(bf16)
            acc[6 + b, h] = jnp.dot(with_ones(ownv[b, h]), p, preferred_element_type=f32)
            md[6 + b, h] = jnp.broadcast_to(m, (8, ROWS))

    forward(0, 1)
    forward(1, 1)
    forward(0, 2)
    forward(1, 2)
    forward(0, 3)
    forward(1, 3)
    forward(2, 1)
    forward(3, 1)
    forward(0, 4)
    forward(1, 4)
    begin(4)
    begin(5)
    for j in range(3):
        xcopies(2 - j)[1].wait_recv()
    tcopy = pltpu.make_async_copy(tbuf, tsm, lsem.at[1])
    tcopy.start()
    for j in (2, 0, 1):
        xcopies(2 - j)[0].wait_recv()
    tcopy.wait()
    for st in range(4):
        settle(0, st)
        settle(1, st)
    for h in range(2):
        for p in range(ZN):
            pair = jnp.concatenate([rv[p, 0, h], rv[p, 1, h]], axis=0).astype(f32)
            rvt[h, :, p * 128 : p * 128 + 128] = jnp.transpose(pair).astype(bf16)

    sbuf, rbuf = (s0, s1), (r0, r1)

    def unit_a(u, h, t, keys, biases):
        q = queries_of(u, h)
        old = md[u, h, 0:1, :]
        top = old
        at = 0
        for k, bias in zip(keys, biases):
            s = scores_of(k, q)
            sbuf[t][at : at + k.shape[0], :] = s
            best = jnp.max(s, axis=0, keepdims=True)
            top = jnp.maximum(top, best if bias is None else best + bias)
            at += k.shape[0]
        md[u, h, 0:1, :] = top
        rbuf[t][0:1, :] = top * C2
        rbuf[t][1:2, :] = jnp.exp2((old - top) * C2)

    def unit_b(u, h, t, vts, biases):
        low, factor = rbuf[t][0:1, :], rbuf[t][1:2, :]
        weights = []
        at = 0
        for vt, bias in zip(vts, biases):
            width = vt.shape[1]
            less = low if bias is None else low - bias
            weights.append(jnp.exp2(sbuf[t][at : at + width, :] * C2 - less).astype(bf16))
            at += width
        p = weights[0] if len(weights) == 1 else jnp.concatenate(weights, axis=0)
        vt = vts[0] if len(vts) == 1 else jnp.concatenate(vts, axis=1)
        acc[u, h] = acc[u, h] * factor + jnp.dot(with_ones(vt), p, preferred_element_type=f32)

    def pipeline(unit_1, unit_2, after=None):
        unit_1(0, 0)

        def body(j, _):
            unit_1(2 * j + 1, 1)
            unit_2(2 * j, 0)
            if after is not None:
                after(2 * j)
            unit_1(2 * j + 2, 0)
            unit_2(2 * j + 1, 1)
            if after is not None:
                after(2 * j + 1)
            return 0

        lax.fori_loop(0, 3, body, 0)
        unit_1(7, 1)
        unit_2(6, 0)
        unit_2(7, 1)

    def root_stage(h):
        def first(u, t):
            unit_a(u, h, t, [jnp.concatenate([rk[p, core, h] for p in range(ZN) for core in range(2)], axis=0)], [None])

        def second(u, t):
            unit_b(u, h, t, [rvt[h]], [None])

        pipeline(first, second)

    def node_stage(h, st, after=None):
        members = [(i, pos, core) for i, pos in enumerate(STAGES[st]) for core in range(2)]

        def names(u):
            got = []
            for i, pos, core in members:
                zz = lax.rem(z + POS_DZ[pos] + ZN, ZN)
                owner = zz * 8 + x * 2 + (c if core == 0 else 1 - c)
                got.append(tsm[u // 2, u % 2, owner])
            biases = [jnp.where(g > 0, 0.0, NEG).astype(f32) for g in got]
            return [jnp.clip(g - 1, 0, SLOTS - 1) for g in got], biases

        def first(u, t):
            at, biases = names(u)
            unit_a(u, h, t, [nodes[h][0][st][i, core, a] for (i, _, core), a in zip(members, at)], biases)

        def second(u, t):
            at, biases = names(u)
            unit_b(u, h, t, [nodes[h][1][st][i, core, a] for (i, _, core), a in zip(members, at)], biases)

        pipeline(first, second, after)

    def three(v):
        a = v.astype(bf16).astype(f32)
        b = (v - a).astype(bf16).astype(f32)
        return [a, b, v - a - b]

    def ocopy(u, h):
        j, b = u // 2, u % 2
        return pltpu.make_async_remote_copy(
            sendbuf.at[h, j, b], recvbuf.at[h, 2 - j, b], osend.at[h, j, b], orecv.at[h, 2 - j, b],
            device_id=dev(dx=j + 1), device_id_type=MESH,
        )

    def send_part(h):
        def after(u):
            j, b = u // 2, u % 2
            sendbuf[h, j, b, :DIM, :] = acc[u, h, :DIM, :].astype(bf16)
            tail = three(md[u, h, 0:1, :]) + three(acc[u, h, DIM : DIM + 1, :])
            tail = jnp.concatenate(tail + [jnp.zeros((TAIL - 6, ROWS), f32)], axis=0)
            sendbuf[h, j, b, DIM:, :] = tail.astype(bf16)
            ocopy(u, h).start()

        return after

    def merge(h):
        for j in range(3):
            for b in range(2):
                ocopy(2 * (2 - j) + b, h).wait_recv()
        for b in range(2):
            tops, dens, sums = [md[6 + b, h, 0:1, :]], [acc[6 + b, h, DIM : DIM + 1, :]], [acc[6 + b, h, :DIM, :]]
            for j in range(3):
                tail = recvbuf[h, j, b, DIM:, :].astype(f32)
                tops.append(tail[0:1] + tail[1:2] + tail[2:3])
                dens.append(tail[3:4] + tail[4:5] + tail[5:6])
                sums.append(recvbuf[h, j, b, :DIM, :].astype(f32))
            top = functools.reduce(jnp.maximum, tops)
            ws = [jnp.exp2((t - top) * C2) for t in tops]
            den = sum(w * d for w, d in zip(ws, dens))
            inv = 1.0 / den
            total = sum(s * (w * inv) for s, w in zip(sums, ws))
            rows = jnp.transpose(total)
            live = lax.broadcasted_iota(jnp.int32, (SEG, DIM), 0) < seg_s[b]
            part = jnp.zeros((SEG, DIM), f32)
            for g in range(GROUP):
                one = jnp.where(live, rows[g * SEG : g * SEG + SEG, :], 0.0)
                att[b, :, h * 1024 + g * 128 : h * 1024 + g * 128 + 128] = one
                part = part + one * one
            part = jnp.broadcast_to(jnp.sum(part, axis=1, keepdims=True), (SEG, DIM))
            ssq[b] = part if h == 0 else ssq[b] + part

    root_stage(0)
    forward(2, 2)
    forward(3, 2)
    root_stage(1)
    forward(2, 3)
    forward(3, 3)
    settle(2, 0)
    settle(3, 0)
    node_stage(0, 0)
    forward(4, 1)
    forward(5, 1)
    forward(2, 4)
    forward(3, 4)
    settle(2, 1)
    settle(3, 1)
    node_stage(0, 1)
    forward(4, 2)
    forward(5, 2)
    settle(2, 2)
    settle(3, 2)
    node_stage(0, 2)
    settle(2, 3)
    settle(3, 3)
    node_stage(0, 3, send_part(0))
    forward(4, 3)
    forward(5, 3)
    settle(4, 0)
    settle(5, 0)
    node_stage(1, 0)
    forward(4, 4)
    forward(5, 4)
    settle(4, 1)
    settle(5, 1)
    node_stage(1, 1)
    settle(4, 2)
    settle(5, 2)
    node_stage(1, 2)
    merge(0)
    settle(4, 3)
    settle(5, 3)
    node_stage(1, 3, send_part(1))
    merge(1)

    def ycopy(d):
        return pltpu.make_async_remote_copy(
            ssq, ssq_in.at[3 - d], ysend.at[d - 1], yrecv.at[3 - d], device_id=dev(dy=d), device_id_type=MESH
        )

    for d in (1, 2, 3):
        go(ycopy(d))
    for d in (1, 2, 3):
        ycopy(d).wait_recv()
    for b in range(2):
        squares = ssq[b] + ssq_in[0, b] + ssq_in[1, b] + ssq_in[2, b]
        scale = lax.rsqrt(squares / (HEADS * DIM) + 1e-6)
        for g in range(2 * GROUP):
            at = slice(g * 128, g * 128 + 128)
            out_ref[b, :, at] = (att[b, :, at] * scale * gain_ref[:, at].astype(f32)).astype(bf16)

    for copy in started:
        copy.wait_send()
    for h in range(2):
        for u in range(6):
            ocopy(u, h).wait_send()


def on_device(queries, root_kv, node_kv, own_kv, anc_owner, anc_slot, depth_len, seg_len, norm_gain):
    bf16, f32 = jnp.bfloat16, jnp.float32

    def rows_of(kv):
        lead = kv.shape[:-2]
        n = len(lead)
        kv = kv.reshape(lead + (2, 2, DIM))
        kv = kv.transpose(tuple(range(n)) + (n + 1, n, n + 2))
        return kv.reshape(-1, DIM)

    vmem = pl.BlockSpec(memory_space=pltpu.VMEM)
    smem = pl.BlockSpec(memory_space=pltpu.SMEM)
    node_refs = [
        pltpu.VMEM((len(members), 2, SLOTS, 128, 128), bf16) for _ in range(4) for members in STAGES
    ]
    dma = pltpu.SemaphoreType.DMA
    scratch = [
        pltpu.VMEM((XN, 2, SEG, 2048), bf16),
        pltpu.VMEM((ZN, 2, 2, ROOT, DIM), bf16),
        pltpu.VMEM((ZN, 2, 2, ROOT, DIM), bf16),
        pltpu.VMEM((2, DIM, ZN * 2 * ROOT), bf16),
        pltpu.VMEM((2, 2, 128, DIM), bf16),
        pltpu.VMEM((2, 2, DIM, 128), bf16),
        *node_refs,
        pltpu.VMEM((8, 2, DIM + TAIL, ROWS), f32),
        pltpu.VMEM((8, 2, 8, ROWS), f32),
        pltpu.VMEM((1024, ROWS), f32),
        pltpu.VMEM((1024, ROWS), f32),
        pltpu.VMEM((8, ROWS), f32),
        pltpu.VMEM((8, ROWS), f32),
        pltpu.VMEM((XN, 8, 128), jnp.int32),
        pltpu.SMEM((XN, 8, 128), jnp.int32),
        pltpu.VMEM((2, 3, 2, DIM + TAIL, ROWS), bf16),
        pltpu.VMEM((2, 3, 2, DIM + TAIL, ROWS), bf16),
        pltpu.VMEM((2, SEG, 2048), f32),
        pltpu.VMEM((2, SEG, DIM), f32),
        pltpu.VMEM((3, 2, SEG, DIM), f32),
        dma((NPIECE, 2, 4)),
        dma((NPIECE, 2, 4)),
        dma((NPIECE, 8)),
        dma((NPIECE, 8)),
        dma((3,)),
        dma((3,)),
        dma((3,)),
        dma((3,)),
        dma((2, 3, 2)),
        dma((2, 3, 2)),
        dma((3,)),
        dma((3,)),
        dma((2,)),
    ]
    return pl.pallas_call(
        kernel,
        out_shape=jax.ShapeDtypeStruct(queries.shape, bf16),
        in_specs=[pl.BlockSpec(memory_space=pl.ANY), vmem, vmem, vmem, smem, smem, smem, smem, vmem],
        out_specs=vmem,
        scratch_shapes=scratch,
        compiler_params=pltpu.CompilerParams(
            collective_id=0, has_side_effects=True, vmem_limit_bytes=48 * 2**20
        ),
        name="tree_attention",
    )(
        queries, rows_of(root_kv), rows_of(node_kv), rows_of(own_kv),
        anc_owner, anc_slot, depth_len, seg_len, norm_gain.reshape(1, -1),
    )


def solution(mesh):
    in_specs = (
        P("branch", None, "blk"),
        P("branch", None, "blk"),
        P("branch", None, None, "blk"),
        P("branch", None, None, "blk"),
        P("branch", None),
        P("branch", None),
        P("branch"),
        P("branch"),
        P("blk"),
    )
    return jax.shard_map(
        on_device, mesh=mesh, in_specs=in_specs, out_specs=P("branch", None, "blk"), check_vma=False
    )
```

```python
import functools
import math

import jax
import jax.numpy as jnp
from jax import lax
from jax.experimental import pallas as pl
from jax.experimental.pallas import tpu as pltpu
from jax.sharding import PartitionSpec as P

MESH = pl.DeviceIdType.MESH
HEADS = 64
DIM = 128
SEG = 32
GROUP = 8
SLOTS = 3
ROWS = GROUP * SEG
ROOT = 64
ZN = 8
XN = 4
C2 = math.log2(math.e) / math.sqrt(DIM)
NEG = -1e30
TAIL = 16
POS_DZ = (0, -1, 1, -2, 2, -3, 3, 4)
STAGES = ((3, 1, 0, 2, 4), (5, 6), (7,))
NEAR = len(STAGES[0])
NPIECE = 6


def pos_of(step, direction):
    return 7 if step == 4 else 2 * step - 1 + direction


def kernel(
    q_hbm, root_hbm, node_hbm, own_hbm, owner_hbm, slot_hbm, depth_hbm, seg_hbm, gain_hbm, out_ref,
    root_x, node_x, own_x, owner_s, slot_s, depth_s, seg_s, gain_ref,
    qbuf, rk, rv, rvt, ownk, ownv,
    n000, n001, n002, n010, n011, n012, n100, n101, n102, n110, n111, n112,
    acc, md, s0, s1, r0, r1, tbuf, tsm, sendbuf, recvbuf, att, ssq, ssq_in,
    zsend, zrecv, csend, crecv, qsend, qrecv, tsend, trecv, osend, orecv, ysend, yrecv, lsem,
):
    bf16, f32 = jnp.bfloat16, jnp.float32
    nodes = (
        ((n000, n001, n002), (n010, n011, n012)),
        ((n100, n101, n102), (n110, n111, n112)),
    )
    y = lax.axis_index("blk")
    r = lax.axis_index("branch")
    z, x, c = r // 8, (r // 2) % 4, r % 2

    def dev(dy=0, dz=0, dx=0, dc=0):
        zz = lax.rem(z + dz + ZN, ZN)
        xx = lax.rem(x + dx + XN, XN)
        cc = lax.rem(c + dc, 2)
        return (lax.rem(y + dy, 4), zz * 8 + xx * 2 + cc)

    bar = pltpu.get_barrier_semaphore()
    peers = [dev(dz=1), dev(dz=-1), dev(dc=1)]
    peers += [dev(dx=d) for d in (1, 2, 3)] + [dev(dy=d) for d in (1, 2, 3)]
    for p in peers:
        pl.semaphore_signal(bar, inc=1, device_id=p, device_id_type=MESH)

    up, down, other = dev(dz=1), dev(dz=-1), dev(dc=1)

    def local(i, src, dst):
        copy = pltpu.make_async_copy(src, dst, lsem.at[i])
        copy.start()
        return copy

    node_in = local(0, node_hbm, node_x)
    root_in = local(1, root_hbm, root_x)
    small_in = [
        local(2, owner_hbm, owner_s), local(3, slot_hbm, slot_s), local(4, depth_hbm, depth_s), local(5, seg_hbm, seg_s)
    ]
    q_in = local(6, q_hbm, qbuf.at[3])
    own_in = local(7, own_hbm, own_x)
    gain_in = local(8, gain_hbm, gain_ref)

    row = lax.broadcasted_iota(jnp.int32, (128, 128), 0)
    col = lax.broadcasted_iota(jnp.int32, (128, 128), 1)
    want = (row % 32) * 4 + row // 32
    pick = jnp.where(col == want, 1.0, 0.0).astype(bf16)

    def apart(ref, first):
        return jnp.dot(pick, ref[first : first + 128, :], preferred_element_type=f32)

    def prepare_root():
        for t in range(2):
            got = apart(root_x, t * 128).astype(bf16)
            for h in range(2):
                rk[0, 0, h, t * 32 : t * 32 + 32, :] = got[h * 64 : h * 64 + 32]
                rv[0, 0, h, t * 32 : t * 32 + 32, :] = got[h * 64 + 32 : h * 64 + 64]

    def prepare_nodes():
        for s in range(SLOTS):
            got = [apart(node_x, (s * 4 + t) * 128) for t in range(4)]
            for h in range(2):
                keys = jnp.concatenate([g[h * 64 : h * 64 + 32] for g in got], axis=0)
                vals = jnp.concatenate([g[h * 64 + 32 : h * 64 + 64] for g in got], axis=0)
                nodes[h][0][0][2, 0, s] = keys.astype(bf16)
                nodes[h][1][0][2, 0, s] = jnp.transpose(vals).astype(bf16)

    def prepare_own():
        zeros96 = jnp.zeros((96, 128), f32)
        for b in range(2):
            got = apart(own_x, b * 128)
            for h in range(2):
                keys = jnp.concatenate([got[h * 64 : h * 64 + 32], zeros96], axis=0)
                vals = jnp.concatenate([got[h * 64 + 32 : h * 64 + 64], zeros96], axis=0)
                ownk[b, h] = keys.astype(bf16)
                ownv[b, h] = jnp.transpose(vals).astype(bf16)

    def prepare_table():
        lane = lax.broadcasted_iota(jnp.int32, (8, 128), 1)
        sub = lax.broadcasted_iota(jnp.int32, (8, 128), 0)
        table = jnp.zeros((8, 128), jnp.int32)
        for b in range(2):
            for l in range(8):
                name = jnp.where(l < depth_s[b], owner_s[b, l], -1)
                code = jnp.where(l < depth_s[b], 4 * owner_s[b, l] + slot_s[b, l] + 1, 0)
                table = jnp.where((lane == name) & (sub == 2 + b), slot_s[b, l] + 1, table)
                table = jnp.where((lane == l) & (sub == b), code, table)
        tbuf[3] = table

    root_in.wait()
    prepare_root()
    node_in.wait()
    prepare_nodes()
    for copy in small_in:
        copy.wait()
    prepare_table()
    q_in.wait()

    pl.semaphore_wait(bar, len(peers))

    def view(piece, pos, core):
        if piece < 2:
            return (rk, rv)[piece].at[pos, core]
        for st, members in enumerate(STAGES):
            if pos in members:
                return nodes[piece // 2 - 1][piece % 2][st].at[members.index(pos), core]

    started = []

    def zcopy(piece, direction, step):
        src = view(piece, 0 if step == 1 else pos_of(step - 1, direction), 0)
        dst = view(piece, pos_of(step, direction), 0)
        return pltpu.make_async_remote_copy(
            src, dst, zsend.at[piece, direction, step - 1], zrecv.at[piece, direction, step - 1],
            device_id=up if direction == 0 else down, device_id_type=MESH,
        )

    def ccopy(piece, pos):
        return pltpu.make_async_remote_copy(
            view(piece, pos, 0), view(piece, pos, 1), csend.at[piece, pos], crecv.at[piece, pos],
            device_id=other, device_id_type=MESH,
        )

    def go(copy):
        copy.start()
        started.append(copy)

    def send_own(kind, which):
        for direction in (0, 1):
            go(zcopy(2 * kind + (which ^ direction), direction, 1))

    def hop(kind, which, step):
        for direction in (0, 1):
            piece = 2 * kind + (which ^ direction)
            zcopy(piece, direction, step).wait_recv()
            if step < 3 or (step == 3 and which == 0):
                go(zcopy(piece, direction, step + 1))
            go(ccopy(piece, pos_of(step, direction)))

    def settle(kind, positions):
        for pos in positions:
            for piece in (2 * kind, 2 * kind + 1):
                ccopy(piece, pos).wait_recv()

    def qcopy(j):
        return pltpu.make_async_remote_copy(
            qbuf.at[3], qbuf.at[2 - j], qsend.at[j], qrecv.at[2 - j], device_id=dev(dx=j + 1), device_id_type=MESH
        )

    def tcopy(j):
        return pltpu.make_async_remote_copy(
            tbuf.at[3], tbuf.at[2 - j], tsend.at[j], trecv.at[2 - j], device_id=dev(dx=j + 1), device_id_type=MESH
        )

    send_own(0, 0)
    send_own(0, 1)
    send_own(1, 0)
    for j in range(3):
        go(tcopy(j))
    for j in (0, 2, 1):
        go(qcopy(j))
    for piece in range(NPIECE):
        go(ccopy(piece, 0))
    own_in.wait()
    prepare_own()
    hop(0, 0, 1)
    hop(0, 1, 1)
    send_own(1, 1)

    def queries_of(u, h):
        j, b = u // 2, u % 2
        parts = [qbuf[j, b, :, h * 1024 + g * 128 : h * 1024 + g * 128 + 128] for g in range(GROUP)]
        return jnp.concatenate(parts, axis=0)

    def scores_of(keys, q):
        return lax.dot_general(keys, q, (((1,), (1,)), ((), ())), preferred_element_type=f32)

    def with_ones(vt):
        return jnp.concatenate([vt, jnp.ones((TAIL, vt.shape[1]), bf16)], axis=0)

    def clear(u, _):
        for h in range(2):
            acc[u, h] = jnp.zeros((DIM + TAIL, ROWS), f32)
            md[u, h] = jnp.full((8, ROWS), NEG, f32)
        return 0

    lax.fori_loop(0, 6, clear, 0)
    key_at = lax.broadcasted_iota(jnp.int32, (128, ROWS), 0)
    query_at = lax.rem(lax.broadcasted_iota(jnp.int32, (128, ROWS), 1), SEG)
    causal = key_at <= query_at
    for b in range(2):
        for h in range(2):
            s = scores_of(ownk[b, h], queries_of(6 + b, h))
            s = jnp.where(causal, s, NEG)
            m = jnp.max(s, axis=0, keepdims=True)
            p = jnp.exp2(s * C2 - m * C2).astype(bf16)
            acc[6 + b, h] = jnp.dot(with_ones(ownv[b, h]), p, preferred_element_type=f32)
            md[6 + b, h] = jnp.broadcast_to(m, (8, ROWS))

    hop(0, 0, 2)
    hop(0, 1, 2)
    send_own(2, 0)
    hop(0, 0, 3)
    hop(0, 1, 3)
    send_own(2, 1)
    hop(1, 0, 1)
    hop(1, 1, 1)
    hop(2, 0, 1)
    for j in range(3):
        tcopy(2 - j).wait_recv()
    t_in = local(9, tbuf, tsm)
    hop(0, 0, 4)
    for j in (2, 0, 1):
        qcopy(2 - j).wait_recv()
    t_in.wait()
    settle(0, range(ZN))
    for h in range(2):
        for p in range(ZN):
            pair = jnp.concatenate([rv[p, 0, h], rv[p, 1, h]], axis=0).astype(f32)
            rvt[h, :, p * 128 : p * 128 + 128] = jnp.transpose(pair).astype(bf16)

    sbuf, rbuf = (s0, s1), (r0, r1)

    def unit_a(u, h, t, keys, biases):
        q = queries_of(u, h)
        old = md[u, h, 0:1, :]
        top = old
        s = scores_of(keys[0] if len(keys) == 1 else jnp.concatenate(keys, axis=0), q)
        sbuf[t][0 : s.shape[0], :] = s
        at = 0
        for k, bias in zip(keys, biases):
            best = jnp.max(s[at : at + k.shape[0]], axis=0, keepdims=True)
            top = jnp.maximum(top, best if bias is None else best + bias)
            at += k.shape[0]
        md[u, h, 0:1, :] = top
        rbuf[t][0:1, :] = top * C2
        rbuf[t][1:2, :] = jnp.exp2((old - top) * C2)

    def unit_b(u, h, t, vts, biases):
        low, factor = rbuf[t][0:1, :], rbuf[t][1:2, :]
        weights = []
        at = 0
        for vt, bias in zip(vts, biases):
            width = vt.shape[1]
            less = low if bias is None else low - bias
            weights.append(jnp.exp2(sbuf[t][at : at + width, :] * C2 - less).astype(bf16))
            at += width
        p = weights[0] if len(weights) == 1 else jnp.concatenate(weights, axis=0)
        vt = vts[0] if len(vts) == 1 else jnp.concatenate(vts, axis=1)
        acc[u, h] = acc[u, h] * factor + jnp.dot(with_ones(vt), p, preferred_element_type=f32)

    def pipeline(unit_1, unit_2, after=None, hooks=()):
        unit_1(0, 0)

        def body(j, _):
            unit_1(2 * j + 1, 1)
            unit_2(2 * j, 0)
            if after is not None:
                after(2 * j)
            unit_1(2 * j + 2, 0)
            unit_2(2 * j + 1, 1)
            if after is not None:
                after(2 * j + 1)
            return 0

        at = 0
        for when, hook in hooks:
            lax.fori_loop(at, when, body, 0)
            hook()
            at = when
        lax.fori_loop(at, 3, body, 0)
        unit_1(7, 1)
        unit_2(6, 0)
        unit_2(7, 1)

    def root_stage(h, hooks=()):
        def first(u, t):
            unit_a(u, h, t, [jnp.concatenate([rk[p, core, h] for p in range(ZN) for core in range(2)], axis=0)], [None])

        def second(u, t):
            unit_b(u, h, t, [rvt[h]], [None])

        pipeline(first, second, None, hooks)

    def bias_of(active):
        return jnp.where(active, 0.0, NEG).astype(f32)

    def near_stage(h, hooks=()):
        def names(u):
            got, biases = [], []
            for l in range(8):
                code = tsm[u // 2, u % 2, l]
                owner = code >> 2
                at = ((owner >> 3) - z + (2 + ZN)) & (ZN - 1)
                core = (owner + c) & 1
                mine = (code > 0) & (((owner >> 1) & (XN - 1)) == x) & (at < NEAR)
                biases.append(bias_of(mine))
                got.append((jnp.clip(at, 0, NEAR - 1), core, jnp.clip((code & 3) - 1, 0, SLOTS - 1)))
            return got, biases

        def first(u, t):
            at, biases = names(u)
            unit_a(u, h, t, [nodes[h][0][0][a] for a in at], biases)

        def second(u, t):
            at, biases = names(u)
            unit_b(u, h, t, [nodes[h][1][0][a] for a in at], biases)

        pipeline(first, second, None, hooks)

    def far_stage(h, st, after=None, hooks=()):
        members = [(i, pos, core) for i, pos in enumerate(STAGES[st]) for core in range(2)]

        def names(u):
            got = []
            for i, pos, core in members:
                zz = lax.rem(z + POS_DZ[pos] + ZN, ZN)
                owner = zz * 8 + x * 2 + (c if core == 0 else 1 - c)
                got.append(tsm[u // 2, 2 + u % 2, owner])
            return [jnp.clip(g - 1, 0, SLOTS - 1) for g in got], [bias_of(g > 0) for g in got]

        def first(u, t):
            at, biases = names(u)
            unit_a(u, h, t, [nodes[h][0][st][i, core, a] for (i, _, core), a in zip(members, at)], biases)

        def second(u, t):
            at, biases = names(u)
            unit_b(u, h, t, [nodes[h][1][st][i, core, a] for (i, _, core), a in zip(members, at)], biases)

        pipeline(first, second, after, hooks)

    def three(v):
        a = v.astype(bf16).astype(f32)
        b = (v - a).astype(bf16).astype(f32)
        return [a, b, v - a - b]

    def ocopy(u, h):
        j, b = u // 2, u % 2
        return pltpu.make_async_remote_copy(
            sendbuf.at[h, j, b], recvbuf.at[h, 2 - j, b], osend.at[h, j, b], orecv.at[h, 2 - j, b],
            device_id=dev(dx=j + 1), device_id_type=MESH,
        )

    def send_part(h):
        def after(u):
            j, b = u // 2, u % 2
            sendbuf[h, j, b, :DIM, :] = acc[u, h, :DIM, :].astype(bf16)
            tail = three(md[u, h, 0:1, :]) + three(acc[u, h, DIM : DIM + 1, :])
            tail = jnp.concatenate(tail + [jnp.zeros((TAIL - 6, ROWS), f32)], axis=0)
            sendbuf[h, j, b, DIM:, :] = tail.astype(bf16)
            ocopy(u, h).start()

        return after

    def merge(h):
        for j in range(3):
            for b in range(2):
                ocopy(2 * (2 - j) + b, h).wait_recv()
        for b in range(2):
            tops, dens, sums = [md[6 + b, h, 0:1, :]], [acc[6 + b, h, DIM : DIM + 1, :]], [acc[6 + b, h, :DIM, :]]
            for j in range(3):
                tail = recvbuf[h, j, b, DIM:, :].astype(f32)
                tops.append(tail[0:1] + tail[1:2] + tail[2:3])
                dens.append(tail[3:4] + tail[4:5] + tail[5:6])
                sums.append(recvbuf[h, j, b, :DIM, :].astype(f32))
            top = functools.reduce(jnp.maximum, tops)
            ws = [jnp.exp2((t - top) * C2) for t in tops]
            den = sum(w * d for w, d in zip(ws, dens))
            inv = 1.0 / den
            total = sum(s * (w * inv) for s, w in zip(sums, ws))
            live = lax.rem(lax.broadcasted_iota(jnp.int32, (1, ROWS), 1), SEG) < seg_s[b]
            total = jnp.where(live, total, 0.0)
            part = jnp.sum(total * total, axis=0, keepdims=True)
            ssq[b : b + 1, :] = part if h == 0 else ssq[b : b + 1, :] + part
            rows = jnp.transpose(total)
            for g in range(GROUP):
                at = h * 1024 + g * 128
                att[b, :, at : at + 128] = rows[g * SEG : g * SEG + SEG, :]

    root_stage(0)
    hop(1, 0, 2)
    root_stage(1, [(1, lambda: hop(1, 1, 2))])
    settle(1, (0, 1, 2, 3, 4))

    def hook_a():
        hop(1, 0, 3)
        hop(2, 1, 1)

    near_stage(0, [(1, hook_a)])
    hop(1, 1, 3)
    settle(1, (5, 6))
    far_stage(0, 1, None, [(1, lambda: hop(2, 0, 2))])
    hop(1, 0, 4)
    settle(1, (7,))
    far_stage(0, 2, send_part(0))
    hop(2, 1, 2)
    settle(2, (0, 1, 2, 3, 4))
    near_stage(1, [(1, lambda: hop(2, 0, 3)), (2, lambda: hop(2, 1, 3))])
    settle(2, (5, 6))
    far_stage(1, 1, None, [(1, lambda: hop(2, 0, 4))])
    settle(2, (7,))
    far_stage(1, 2, send_part(1))
    merge(0)
    merge(1)

    def ycopy(d):
        return pltpu.make_async_remote_copy(
            ssq, ssq_in.at[3 - d], ysend.at[d - 1], yrecv.at[3 - d], device_id=dev(dy=d), device_id_type=MESH
        )

    for d in (1, 2, 3):
        go(ycopy(d))
    for d in (1, 2, 3):
        ycopy(d).wait_recv()
    gain_in.wait()
    squares = jnp.transpose(ssq[...] + ssq_in[0] + ssq_in[1] + ssq_in[2])
    squares = sum(squares[g * SEG : g * SEG + SEG, :] for g in range(GROUP))
    scales = lax.rsqrt(squares / (HEADS * DIM) + 1e-6)
    for b in range(2):
        scale = scales[:, b : b + 1]
        for g in range(2 * GROUP):
            at = slice(g * 128, g * 128 + 128)
            out_ref[b, :, at] = (att[b, :, at] * scale * gain_ref[at].astype(f32).reshape(1, DIM)).astype(bf16)

    for copy in started:
        copy.wait_send()
    for h in range(2):
        for u in range(6):
            ocopy(u, h).wait_send()


def on_device(queries, root_kv, node_kv, own_kv, anc_owner, anc_slot, depth_len, seg_len, norm_gain):
    bf16, f32 = jnp.bfloat16, jnp.float32

    def rows_of(kv):
        lead = kv.shape[:-2]
        n = len(lead)
        kv = kv.reshape(lead + (2, 2, DIM))
        kv = kv.transpose(tuple(range(n)) + (n + 1, n, n + 2))
        return kv.reshape(-1, DIM)

    node_refs = [
        pltpu.VMEM((len(members), 2, SLOTS, 128, 128), bf16) for _ in range(4) for members in STAGES
    ]
    dma = pltpu.SemaphoreType.DMA
    scratch = [
        pltpu.VMEM((2 * 2 * ROOT, DIM), bf16),
        pltpu.VMEM((SLOTS * 2 * 2 * 128, DIM), bf16),
        pltpu.VMEM((2 * 2 * 2 * SEG, DIM), bf16),
        pltpu.SMEM((2, 8), jnp.int32),
        pltpu.SMEM((2, 8), jnp.int32),
        pltpu.SMEM((2,), jnp.int32),
        pltpu.SMEM((2,), jnp.int32),
        pltpu.VMEM((2048,), bf16),
        pltpu.VMEM((XN, 2, SEG, 2048), bf16),
        pltpu.VMEM((ZN, 2, 2, ROOT, DIM), bf16),
        pltpu.VMEM((ZN, 2, 2, ROOT, DIM), bf16),
        pltpu.VMEM((2, DIM, ZN * 2 * ROOT), bf16),
        pltpu.VMEM((2, 2, 128, DIM), bf16),
        pltpu.VMEM((2, 2, DIM, 128), bf16),
        *node_refs,
        pltpu.VMEM((8, 2, DIM + TAIL, ROWS), f32),
        pltpu.VMEM((8, 2, 8, ROWS), f32),
        pltpu.VMEM((1024, ROWS), f32),
        pltpu.VMEM((1024, ROWS), f32),
        pltpu.VMEM((8, ROWS), f32),
        pltpu.VMEM((8, ROWS), f32),
        pltpu.VMEM((XN, 8, 128), jnp.int32),
        pltpu.SMEM((XN, 8, 128), jnp.int32),
        pltpu.VMEM((2, 3, 2, DIM + TAIL, ROWS), bf16),
        pltpu.VMEM((2, 3, 2, DIM + TAIL, ROWS), bf16),
        pltpu.VMEM((2, SEG, 2048), f32),
        pltpu.VMEM((8, ROWS), f32),
        pltpu.VMEM((3, 8, ROWS), f32),
        dma((NPIECE, 2, 4)),
        dma((NPIECE, 2, 4)),
        dma((NPIECE, 8)),
        dma((NPIECE, 8)),
        dma((3,)),
        dma((3,)),
        dma((3,)),
        dma((3,)),
        dma((2, 3, 2)),
        dma((2, 3, 2)),
        dma((3,)),
        dma((3,)),
        dma((10,)),
    ]
    return pl.pallas_call(
        kernel,
        out_shape=jax.ShapeDtypeStruct(queries.shape, bf16),
        in_specs=[pl.BlockSpec(memory_space=pltpu.HBM)] * 9,
        out_specs=pl.BlockSpec(memory_space=pltpu.VMEM),
        scratch_shapes=scratch,
        compiler_params=pltpu.CompilerParams(
            collective_id=0, has_side_effects=True, vmem_limit_bytes=64 * 2**20
        ),
        name="tree_attention",
    )(
        queries, rows_of(root_kv), rows_of(node_kv), rows_of(own_kv),
        anc_owner, anc_slot, depth_len, seg_len, norm_gain,
    )


def solution(mesh):
    in_specs = (
        P("branch", None, "blk"),
        P("branch", None, "blk"),
        P("branch", None, None, "blk"),
        P("branch", None, None, "blk"),
        P("branch", None),
        P("branch", None),
        P("branch"),
        P("branch"),
        P("blk"),
    )
    return jax.shard_map(
        on_device, mesh=mesh, in_specs=in_specs, out_specs=P("branch", None, "blk"), check_vma=False
    )
```

```python
import functools
import math

import jax
import jax.numpy as jnp
from jax import lax
from jax.experimental import pallas as pl
from jax.experimental.pallas import tpu as pltpu
from jax.sharding import PartitionSpec as P

MESH = pl.DeviceIdType.MESH
HEADS = 64
DIM = 128
SEG = 32
GROUP = 8
SLOTS = 3
ROWS = GROUP * SEG
ROOT = 64
ZN = 8
XN = 4
C2 = math.log2(math.e) / math.sqrt(DIM)
NEG = -1e30
TAIL = 16
POS_DZ = (0, -1, 1, -2, 2, -3, 3, 4)
SLOT_DX = (2, 1, 3)
NPIECE = 6


def pos_of(step, direction):
    return 7 if step == 4 else 2 * step - 1 + direction


def kernel(
    q_hbm, root_hbm, node_hbm, own_hbm, owner_hbm, slot_hbm, depth_hbm, seg_hbm, gain_hbm, out_ref,
    root_x, node_x, own_x, owner_s, slot_s, depth_s, seg_s, gain_ref,
    qbuf, rk, rv, rvt, ownk, ownv,
    n00, n01, n10, n11,
    acc, md, s0, s1, r0, r1, tbuf, tsm, sendbuf, recvbuf, att, ssq, ssq_in,
    zsend, zrecv, csend, crecv, qsend, qrecv, tsend, trecv, osend, orecv, ysend, yrecv, lsem,
):
    bf16, f32 = jnp.bfloat16, jnp.float32
    nodes = ((n00, n01), (n10, n11))
    y = lax.axis_index("blk")
    r = lax.axis_index("branch")
    z, x, c = r // 8, (r // 2) % 4, r % 2

    def dev(dy=0, dz=0, dx=0, dc=0):
        zz = lax.rem(z + dz + ZN, ZN)
        xx = lax.rem(x + dx + XN, XN)
        cc = lax.rem(c + dc, 2)
        return (lax.rem(y + dy, 4), zz * 8 + xx * 2 + cc)

    bar = pltpu.get_barrier_semaphore()
    peers = [dev(dz=1), dev(dz=-1), dev(dc=1)]
    peers += [dev(dx=d) for d in (1, 2, 3)] + [dev(dy=d) for d in (1, 2, 3)]
    for p in peers:
        pl.semaphore_signal(bar, inc=1, device_id=p, device_id_type=MESH)

    up, down, other = dev(dz=1), dev(dz=-1), dev(dc=1)

    def local(i, src, dst):
        copy = pltpu.make_async_copy(src, dst, lsem.at[i])
        copy.start()
        return copy

    node_in = local(0, node_hbm, node_x)
    root_in = local(1, root_hbm, root_x)
    small_in = [
        local(2, owner_hbm, owner_s), local(3, slot_hbm, slot_s), local(4, depth_hbm, depth_s), local(5, seg_hbm, seg_s)
    ]
    q_in = local(6, q_hbm, qbuf.at[pl.ds(6, 2)])
    own_in = local(7, own_hbm, own_x)
    gain_in = local(8, gain_hbm, gain_ref)

    row = lax.broadcasted_iota(jnp.int32, (128, 128), 0)
    col = lax.broadcasted_iota(jnp.int32, (128, 128), 1)
    want = (row % 32) * 4 + row // 32
    pick = jnp.where(col == want, 1.0, 0.0).astype(bf16)

    def apart(ref, first):
        return jnp.dot(pick, ref[first : first + 128, :], preferred_element_type=f32)

    def prepare_root():
        for t in range(2):
            got = apart(root_x, t * 128).astype(bf16)
            for h in range(2):
                rk[0, 0, h, t * 32 : t * 32 + 32, :] = got[h * 64 : h * 64 + 32]
                rv[0, 0, h, t * 32 : t * 32 + 32, :] = got[h * 64 + 32 : h * 64 + 64]

    def prepare_nodes(keys_of, values_of):
        for s in range(SLOTS):
            got = [apart(node_x, (s * 4 + t) * 128) for t in range(4)]
            for h in keys_of:
                keys = jnp.concatenate([g[h * 64 : h * 64 + 32] for g in got], axis=0)
                nodes[h][0][0, 0, s] = keys.astype(bf16)
            for h in values_of:
                vals = jnp.concatenate([g[h * 64 + 32 : h * 64 + 64] for g in got], axis=0)
                nodes[h][1][0, 0, s] = jnp.transpose(vals).astype(bf16)

    def prepare_own():
        zeros96 = jnp.zeros((96, 128), f32)
        for b in range(2):
            got = apart(own_x, b * 128)
            for h in range(2):
                keys = jnp.concatenate([got[h * 64 : h * 64 + 32], zeros96], axis=0)
                vals = jnp.concatenate([got[h * 64 + 32 : h * 64 + 64], zeros96], axis=0)
                ownk[b, h] = keys.astype(bf16)
                ownv[b, h] = jnp.transpose(vals).astype(bf16)

    def prepare_table():
        lane = lax.broadcasted_iota(jnp.int32, (8, 128), 1)
        sub = lax.broadcasted_iota(jnp.int32, (8, 128), 0)
        table = jnp.zeros((8, 128), jnp.int32)
        for b in range(2):
            for l in range(8):
                code = jnp.where(l < depth_s[b], 4 * owner_s[b, l] + slot_s[b, l] + 1, 0)
                table = jnp.where((lane == l) & (sub == b), code, table)
        tbuf[3] = table

    root_in.wait()
    prepare_root()
    node_in.wait()
    prepare_nodes((0, 1), (0,))

    pl.semaphore_wait(bar, len(peers))

    def view(piece, pos, core):
        if piece < 2:
            return (rk, rv)[piece].at[pos, core]
        return nodes[piece // 2 - 1][piece % 2].at[POS_DZ[pos] % ZN, core]

    started = []

    def zcopy(piece, direction, step):
        src = view(piece, 0 if step == 1 else pos_of(step - 1, direction), 0)
        dst = view(piece, pos_of(step, direction), 0)
        return pltpu.make_async_remote_copy(
            src, dst, zsend.at[piece, direction, step - 1], zrecv.at[piece, direction, step - 1],
            device_id=up if direction == 0 else down, device_id_type=MESH,
        )

    def ccopy(piece, pos):
        return pltpu.make_async_remote_copy(
            view(piece, pos, 0), view(piece, pos, 1), csend.at[piece, pos], crecv.at[piece, pos],
            device_id=other, device_id_type=MESH,
        )

    def go(copy):
        copy.start()
        started.append(copy)

    def send_own(kind, which):
        for direction in (0, 1):
            go(zcopy(2 * kind + (which ^ direction), direction, 1))

    def hop(kind, which, step):
        for direction in (0, 1):
            piece = 2 * kind + (which ^ direction)
            zcopy(piece, direction, step).wait_recv()
            if step < 3 or (step == 3 and which == 0):
                go(zcopy(piece, direction, step + 1))
            go(ccopy(piece, pos_of(step, direction)))

    def settle(kind, positions):
        for pos in positions:
            for piece in (2 * kind, 2 * kind + 1):
                ccopy(piece, pos).wait_recv()

    def slot_dx(j):
        return jnp.where(j == 0, 2, 2 * j - 1)

    def slot_there(j):
        return lax.rem(3 - j, 3)

    def split(u):
        return jnp.where(u < 6, lax.rem(u, 3), 3), jnp.where(u < 6, lax.div(u, 3), u - 6)

    def qcopy(j, b):
        there = (3 - j) % 3
        return pltpu.make_async_remote_copy(
            qbuf.at[6 + b], qbuf.at[3 * b + there], qsend.at[j, b], qrecv.at[there, b],
            device_id=dev(dx=SLOT_DX[j]), device_id_type=MESH,
        )

    def tcopy(j):
        there = (3 - j) % 3
        return pltpu.make_async_remote_copy(
            tbuf.at[3], tbuf.at[there], tsend.at[j], trecv.at[there], device_id=dev(dx=SLOT_DX[j]), device_id_type=MESH
        )

    send_own(0, 0)
    send_own(0, 1)
    send_own(1, 0)
    q_in.wait()
    for j in (1, 2, 0):
        for b in range(2):
            go(qcopy(j, b))
    for piece in range(4):
        go(ccopy(piece, 0))
    for copy in small_in:
        copy.wait()
    prepare_table()
    for j in range(3):
        go(tcopy(j))
    hop(0, 0, 1)
    hop(0, 1, 1)
    send_own(1, 1)
    prepare_nodes((), (1,))
    go(ccopy(4, 0))
    go(ccopy(5, 0))
    own_in.wait()
    prepare_own()
    hop(0, 0, 2)
    hop(0, 1, 2)
    send_own(2, 0)

    def queries_of(u, h):
        parts = [qbuf[u, :, h * 1024 + g * 128 : h * 1024 + g * 128 + 128] for g in range(GROUP)]
        return jnp.concatenate(parts, axis=0)

    def scores_of(keys, q):
        return lax.dot_general(keys, q, (((1,), (1,)), ((), ())), preferred_element_type=f32)

    def with_ones(vt):
        return jnp.concatenate([vt, jnp.ones((TAIL, vt.shape[1]), bf16)], axis=0)

    def clear(u, _):
        for h in range(2):
            acc[u, h] = jnp.zeros((DIM + TAIL, ROWS), f32)
            md[u, h] = jnp.full((8, ROWS), NEG, f32)
        return 0

    lax.fori_loop(0, 6, clear, 0)
    key_at = lax.broadcasted_iota(jnp.int32, (128, ROWS), 0)
    query_at = lax.rem(lax.broadcasted_iota(jnp.int32, (128, ROWS), 1), SEG)
    causal = key_at <= query_at
    for b in range(2):
        for h in range(2):
            s = scores_of(ownk[b, h], queries_of(6 + b, h))
            s = jnp.where(causal, s, NEG)
            m = jnp.max(s, axis=0, keepdims=True)
            p = jnp.exp2(s * C2 - m * C2).astype(bf16)
            acc[6 + b, h] = jnp.dot(with_ones(ownv[b, h]), p, preferred_element_type=f32)
            md[6 + b, h] = jnp.broadcast_to(m, (8, ROWS))

    hop(0, 0, 3)
    hop(0, 1, 3)
    send_own(2, 1)
    hop(1, 0, 1)
    hop(1, 1, 1)
    for j in range(3):
        tcopy((3 - j) % 3).wait_recv()
    t_in = local(9, tbuf, tsm)
    hop(0, 0, 4)
    hop(2, 0, 1)
    for j in range(3):
        for b in range(2):
            qcopy((3 - j) % 3, b).wait_recv()
    t_in.wait()
    settle(0, range(ZN))
    for h in range(2):
        for p in range(ZN):
            pair = jnp.concatenate([rv[p, 0, h], rv[p, 1, h]], axis=0).astype(f32)
            rvt[h, :, p * 128 : p * 128 + 128] = jnp.transpose(pair).astype(bf16)

    sbuf, rbuf = (s0, s1), (r0, r1)

    def unit_a(u, h, t, keys, biases):
        q = queries_of(u, h)
        old = md[u, h, 0:1, :]
        top = old
        for i in range(0, len(keys), 2):
            s = scores_of(jnp.concatenate(keys[i : i + 2], axis=0), q)
            sbuf[t][i * 128 : i * 128 + 256, :] = s
            for n in range(2):
                best = jnp.max(s[n * 128 : n * 128 + 128], axis=0, keepdims=True)
                top = jnp.maximum(top, best if biases is None else best + biases[i + n])
        md[u, h, 0:1, :] = top
        rbuf[t][0:1, :] = top * C2
        rbuf[t][1:2, :] = jnp.exp2((old - top) * C2)

    def unit_b(u, h, t, vts, biases):
        low, factor = rbuf[t][0:1, :], rbuf[t][1:2, :]
        weights = []
        for i in range(8):
            less = low if biases is None else low - biases[i]
            weights.append(jnp.exp2(sbuf[t][i * 128 : i * 128 + 128, :] * C2 - less).astype(bf16))
        p = jnp.concatenate(weights, axis=0)
        vt = vts[0] if len(vts) == 1 else jnp.concatenate(vts, axis=1)
        acc[u, h] = acc[u, h] * factor + jnp.dot(with_ones(vt), p, preferred_element_type=f32)

    def pipeline(unit_1, unit_2, after=None, hooks=()):
        unit_1(0, 0)

        def body(j, _):
            unit_1(2 * j + 1, 1)
            unit_2(2 * j, 0)
            if after is not None:
                after(2 * j)
            unit_1(2 * j + 2, 0)
            unit_2(2 * j + 1, 1)
            if after is not None:
                after(2 * j + 1)
            return 0

        at = 0
        for when, hook in hooks:
            lax.fori_loop(at, when, body, 0)
            hook()
            at = when
        lax.fori_loop(at, 3, body, 0)
        unit_1(7, 1)
        unit_2(6, 0)
        unit_2(7, 1)

    def root_stage(h, hooks=()):
        def first(u, t):
            unit_a(u, h, t, [jnp.concatenate([rk[p, 0, h], rk[p, 1, h]], axis=0) for p in range(ZN)], None)

        def second(u, t):
            unit_b(u, h, t, [rvt[h]], None)

        pipeline(first, second, None, hooks)

    def bias_of(active):
        return jnp.where(active, 0.0, NEG).astype(f32)

    def node_stage(h, after=None, hooks=()):
        def names(u):
            j, b = split(u)
            got, biases = [], []
            for l in range(8):
                code = tsm[j, b, l]
                owner = code >> 2
                at = ((owner >> 3) - z + ZN) & (ZN - 1)
                core = (owner + c) & 1
                mine = (code > 0) & (((owner >> 1) & (XN - 1)) == x)
                biases.append(bias_of(mine))
                got.append((at, core, jnp.clip((code & 3) - 1, 0, SLOTS - 1)))
            return got, biases

        def first(u, t):
            at, biases = names(u)
            unit_a(u, h, t, [nodes[h][0][a] for a in at], biases)

        def second(u, t):
            at, biases = names(u)
            unit_b(u, h, t, [nodes[h][1][a] for a in at], biases)

        pipeline(first, second, after, hooks)

    def three(v):
        a = v.astype(bf16).astype(f32)
        b = (v - a).astype(bf16).astype(f32)
        return [a, b, v - a - b]

    def ocopy(j, b, h):
        there = slot_there(j)
        return pltpu.make_async_remote_copy(
            sendbuf.at[h, j, b], recvbuf.at[h, there, b], osend.at[h, j, b], orecv.at[h, there, b],
            device_id=dev(dx=slot_dx(j)), device_id_type=MESH,
        )

    def send_part(h):
        def after(u):
            j, b = split(u)
            sendbuf[h, j, b, :DIM, :] = acc[u, h, :DIM, :].astype(bf16)
            tail = three(md[u, h, 0:1, :]) + three(acc[u, h, DIM : DIM + 1, :])
            tail = jnp.concatenate(tail + [jnp.zeros((TAIL - 6, ROWS), f32)], axis=0)
            sendbuf[h, j, b, DIM:, :] = tail.astype(bf16)
            ocopy(j, b, h).start()

        return after

    def merge(h):
        for b in range(2):
            for j in range(3):
                ocopy((3 - j) % 3, b, h).wait_recv()
            tops, dens, sums = [md[6 + b, h, 0:1, :]], [acc[6 + b, h, DIM : DIM + 1, :]], [acc[6 + b, h, :DIM, :]]
            for j in range(3):
                tail = recvbuf[h, j, b, DIM:, :].astype(f32)
                tops.append(tail[0:1] + tail[1:2] + tail[2:3])
                dens.append(tail[3:4] + tail[4:5] + tail[5:6])
                sums.append(recvbuf[h, j, b, :DIM, :].astype(f32))
            top = functools.reduce(jnp.maximum, tops)
            ws = [jnp.exp2((t - top) * C2) for t in tops]
            den = sum(w * d for w, d in zip(ws, dens))
            inv = 1.0 / den
            total = sum(s * (w * inv) for s, w in zip(sums, ws))
            live = lax.rem(lax.broadcasted_iota(jnp.int32, (1, ROWS), 1), SEG) < seg_s[b]
            total = jnp.where(live, total, 0.0)
            part = jnp.sum(total * total, axis=0, keepdims=True)
            ssq[b : b + 1, :] = part if h == 0 else ssq[b : b + 1, :] + part
            rows = jnp.transpose(total)
            for g in range(GROUP):
                at = h * 1024 + g * 128
                att[b, :, at : at + 128] = rows[g * SEG : g * SEG + SEG, :]

    root_stage(0)
    root_stage(1, [(1, lambda: hop(1, 0, 2)), (2, lambda: hop(1, 1, 2))])
    hop(1, 0, 3)
    hop(2, 1, 1)
    hop(2, 0, 2)
    hop(1, 1, 3)
    hop(1, 0, 4)
    hop(2, 1, 2)
    settle(1, range(ZN))
    node_stage(0, send_part(0), [(2, lambda: hop(2, 0, 3))])
    hop(2, 1, 3)
    hop(2, 0, 4)
    settle(2, range(ZN))
    node_stage(1, send_part(1))
    merge(0)
    merge(1)

    def ycopy(d):
        return pltpu.make_async_remote_copy(
            ssq, ssq_in.at[3 - d], ysend.at[d - 1], yrecv.at[3 - d], device_id=dev(dy=d), device_id_type=MESH
        )

    for d in (1, 2, 3):
        go(ycopy(d))
    for d in (1, 2, 3):
        ycopy(d).wait_recv()
    gain_in.wait()
    squares = jnp.transpose(ssq[...] + ssq_in[0] + ssq_in[1] + ssq_in[2])
    squares = sum(squares[g * SEG : g * SEG + SEG, :] for g in range(GROUP))
    scales = lax.rsqrt(squares / (HEADS * DIM) + 1e-6)
    for b in range(2):
        scale = scales[:, b : b + 1]
        for g in range(2 * GROUP):
            at = slice(g * 128, g * 128 + 128)
            out_ref[b, :, at] = (att[b, :, at] * scale * gain_ref[at].astype(f32).reshape(1, DIM)).astype(bf16)

    for copy in started:
        copy.wait_send()
    for h in range(2):
        for j in range(3):
            for b in range(2):
                ocopy(j, b, h).wait_send()


def on_device(queries, root_kv, node_kv, own_kv, anc_owner, anc_slot, depth_len, seg_len, norm_gain):
    bf16, f32 = jnp.bfloat16, jnp.float32

    def rows_of(kv):
        lead = kv.shape[:-2]
        n = len(lead)
        kv = kv.reshape(lead + (2, 2, DIM))
        kv = kv.transpose(tuple(range(n)) + (n + 1, n, n + 2))
        return kv.reshape(-1, DIM)

    node_refs = [pltpu.VMEM((ZN, 2, SLOTS, 128, 128), bf16) for _ in range(4)]
    dma = pltpu.SemaphoreType.DMA
    scratch = [
        pltpu.VMEM((2 * 2 * ROOT, DIM), bf16),
        pltpu.VMEM((SLOTS * 2 * 2 * 128, DIM), bf16),
        pltpu.VMEM((2 * 2 * 2 * SEG, DIM), bf16),
        pltpu.SMEM((2, 8), jnp.int32),
        pltpu.SMEM((2, 8), jnp.int32),
        pltpu.SMEM((2,), jnp.int32),
        pltpu.SMEM((2,), jnp.int32),
        pltpu.VMEM((2048,), bf16),
        pltpu.VMEM((2 * XN, SEG, 2048), bf16),
        pltpu.VMEM((ZN, 2, 2, ROOT, DIM), bf16),
        pltpu.VMEM((ZN, 2, 2, ROOT, DIM), bf16),
        pltpu.VMEM((2, DIM, ZN * 2 * ROOT), bf16),
        pltpu.VMEM((2, 2, 128, DIM), bf16),
        pltpu.VMEM((2, 2, DIM, 128), bf16),
        *node_refs,
        pltpu.VMEM((8, 2, DIM + TAIL, ROWS), f32),
        pltpu.VMEM((8, 2, 8, ROWS), f32),
        pltpu.VMEM((1024, ROWS), f32),
        pltpu.VMEM((1024, ROWS), f32),
        pltpu.VMEM((8, ROWS), f32),
        pltpu.VMEM((8, ROWS), f32),
        pltpu.VMEM((XN, 8, 128), jnp.int32),
        pltpu.SMEM((XN, 8, 128), jnp.int32),
        pltpu.VMEM((2, 3, 2, DIM + TAIL, ROWS), bf16),
        pltpu.VMEM((2, 3, 2, DIM + TAIL, ROWS), bf16),
        pltpu.VMEM((2, SEG, 2048), f32),
        pltpu.VMEM((8, ROWS), f32),
        pltpu.VMEM((3, 8, ROWS), f32),
        dma((NPIECE, 2, 4)),
        dma((NPIECE, 2, 4)),
        dma((NPIECE, 8)),
        dma((NPIECE, 8)),
        dma((3, 2)),
        dma((3, 2)),
        dma((3,)),
        dma((3,)),
        dma((2, 3, 2)),
        dma((2, 3, 2)),
        dma((3,)),
        dma((3,)),
        dma((10,)),
    ]
    return pl.pallas_call(
        kernel,
        out_shape=jax.ShapeDtypeStruct(queries.shape, bf16),
        in_specs=[pl.BlockSpec(memory_space=pltpu.HBM)] * 9,
        out_specs=pl.BlockSpec(memory_space=pltpu.VMEM),
        scratch_shapes=scratch,
        compiler_params=pltpu.CompilerParams(
            collective_id=0, has_side_effects=True, vmem_limit_bytes=64 * 2**20
        ),
        name="tree_attention",
    )(
        queries, rows_of(root_kv), rows_of(node_kv), rows_of(own_kv),
        anc_owner, anc_slot, depth_len, seg_len, norm_gain,
    )


def solution(mesh):
    in_specs = (
        P("branch", None, "blk"),
        P("branch", None, "blk"),
        P("branch", None, None, "blk"),
        P("branch", None, None, "blk"),
        P("branch", None),
        P("branch", None),
        P("branch"),
        P("branch"),
        P("blk"),
    )
    return jax.shard_map(
        on_device, mesh=mesh, in_specs=in_specs, out_specs=P("branch", None, "blk"), check_vma=False
    )
```

```python
import functools
import math

import jax
import jax.numpy as jnp
from jax import lax
from jax.experimental import pallas as pl
from jax.experimental.pallas import tpu as pltpu
from jax.sharding import PartitionSpec as P

MESH = pl.DeviceIdType.MESH
HEADS = 64
DIM = 128
SEG = 32
GROUP = 8
SLOTS = 3
ROWS = GROUP * SEG
ROOT = 64
ZN = 8
XN = 4
C2 = math.log2(math.e) / math.sqrt(DIM)
NEG = -1e30
TAIL = 16
POS_DZ = (0, -1, 1, -2, 2, -3, 3, 4)
SLOT_DX = (2, 1, 3)
NPIECE = 6


def pos_of(step, direction):
    return 7 if step == 4 else 2 * step - 1 + direction


def kernel(
    q_hbm, root_hbm, node_hbm, own_hbm, owner_hbm, slot_hbm, depth_hbm, seg_hbm, gain_hbm, out_ref,
    root_x, node_x, own_x, owner_s, slot_s, depth_s, seg_s, gain_ref,
    qbuf, rk, rv, rvt, ownk, ownv,
    n00, n01, n10, n11,
    acc, md, s0, s1, r0, r1, tbuf, tsm, sendbuf, recvbuf, att, ssq, ssq_in,
    zsend, zrecv, csend, crecv, qsend, qrecv, tsend, trecv, osend, orecv, ysend, yrecv, lsem,
):
    bf16, f32 = jnp.bfloat16, jnp.float32
    nodes = ((n00, n01), (n10, n11))
    y = lax.axis_index("blk")
    r = lax.axis_index("branch")
    z, x, c = r // 8, (r // 2) % 4, r % 2

    def dev(dy=0, dz=0, dx=0, dc=0):
        zz = lax.rem(z + dz + ZN, ZN)
        xx = lax.rem(x + dx + XN, XN)
        cc = lax.rem(c + dc, 2)
        return (lax.rem(y + dy, 4), zz * 8 + xx * 2 + cc)

    bar = pltpu.get_barrier_semaphore()
    peers = [dev(dz=1), dev(dz=-1), dev(dc=1)]
    peers += [dev(dx=d) for d in (1, 2, 3)] + [dev(dy=d) for d in (1, 2, 3)]
    for p in peers:
        pl.semaphore_signal(bar, inc=1, device_id=p, device_id_type=MESH)

    up, down, other = dev(dz=1), dev(dz=-1), dev(dc=1)

    def local(i, src, dst):
        copy = pltpu.make_async_copy(src, dst, lsem.at[i])
        copy.start()
        return copy

    node_in = local(0, node_hbm, node_x)
    root_in = local(1, root_hbm, root_x)
    small_in = [
        local(2, owner_hbm, owner_s), local(3, slot_hbm, slot_s), local(4, depth_hbm, depth_s), local(5, seg_hbm, seg_s)
    ]
    q_in = local(6, q_hbm, qbuf.at[pl.ds(6, 2)])
    own_in = local(7, own_hbm, own_x)
    gain_in = local(8, gain_hbm, gain_ref)

    row = lax.broadcasted_iota(jnp.int32, (128, 128), 0)
    col = lax.broadcasted_iota(jnp.int32, (128, 128), 1)
    want = (row % 32) * 4 + row // 32
    pick = jnp.where(col == want, 1.0, 0.0).astype(bf16)

    def apart(ref, first):
        return jnp.dot(pick, ref[first : first + 128, :], preferred_element_type=f32)

    def prepare_root():
        for t in range(2):
            got = apart(root_x, t * 128).astype(bf16)
            for h in range(2):
                rk[0, 0, h, t * 32 : t * 32 + 32, :] = got[h * 64 : h * 64 + 32]
                rv[0, 0, h, t * 32 : t * 32 + 32, :] = got[h * 64 + 32 : h * 64 + 64]

    def prepare_nodes(keys_of, values_of):
        for s in range(SLOTS):
            got = [apart(node_x, (s * 4 + t) * 128) for t in range(4)]
            for h in keys_of:
                keys = jnp.concatenate([g[h * 64 : h * 64 + 32] for g in got], axis=0)
                nodes[h][0][0, 0, s] = keys.astype(bf16)
            for h in values_of:
                vals = jnp.concatenate([g[h * 64 + 32 : h * 64 + 64] for g in got], axis=0)
                nodes[h][1][0, 0, s] = jnp.transpose(vals).astype(bf16)

    def prepare_own():
        zeros96 = jnp.zeros((96, 128), f32)
        for b in range(2):
            got = apart(own_x, b * 128)
            for h in range(2):
                keys = jnp.concatenate([got[h * 64 : h * 64 + 32], zeros96], axis=0)
                vals = jnp.concatenate([got[h * 64 + 32 : h * 64 + 64], zeros96], axis=0)
                ownk[b, h] = keys.astype(bf16)
                ownv[b, h] = jnp.transpose(vals).astype(bf16)

    def prepare_table():
        lane = lax.broadcasted_iota(jnp.int32, (8, 128), 1)
        sub = lax.broadcasted_iota(jnp.int32, (8, 128), 0)
        table = jnp.zeros((8, 128), jnp.int32)
        for b in range(2):
            for l in range(8):
                code = jnp.where(l < depth_s[b], 4 * owner_s[b, l] + slot_s[b, l] + 1, 0)
                table = jnp.where((lane == l) & (sub == b), code, table)
        tbuf[3] = table

    root_in.wait()
    prepare_root()
    pl.semaphore_wait(bar, len(peers))

    def view(piece, pos, core):
        if piece < 2:
            return (rk, rv)[piece].at[pos, core]
        return nodes[piece // 2 - 1][piece % 2].at[POS_DZ[pos] % ZN, core]

    started = []

    def zcopy(piece, direction, step):
        src = view(piece, 0 if step == 1 else pos_of(step - 1, direction), 0)
        dst = view(piece, pos_of(step, direction), 0)
        return pltpu.make_async_remote_copy(
            src, dst, zsend.at[piece, direction, step - 1], zrecv.at[piece, direction, step - 1],
            device_id=up if direction == 0 else down, device_id_type=MESH,
        )

    def ccopy(piece, pos):
        return pltpu.make_async_remote_copy(
            view(piece, pos, 0), view(piece, pos, 1), csend.at[piece, pos], crecv.at[piece, pos],
            device_id=other, device_id_type=MESH,
        )

    def go(copy):
        copy.start()
        started.append(copy)

    def send_own(kind, which):
        for direction in (0, 1):
            go(zcopy(2 * kind + (which ^ direction), direction, 1))

    def hop(kind, which, step):
        for direction in (0, 1):
            piece = 2 * kind + (which ^ direction)
            zcopy(piece, direction, step).wait_recv()
            if step < 3 or (step == 3 and which == 0):
                go(zcopy(piece, direction, step + 1))
            go(ccopy(piece, pos_of(step, direction)))

    def settle(kind, positions):
        for pos in positions:
            for piece in (2 * kind, 2 * kind + 1):
                ccopy(piece, pos).wait_recv()

    def slot_dx(j):
        return jnp.where(j == 0, 2, 2 * j - 1)

    def slot_there(j):
        return lax.rem(3 - j, 3)

    def split(u):
        return jnp.where(u < 6, lax.rem(u, 3), 3), jnp.where(u < 6, lax.div(u, 3), u - 6)

    def qcopy(j, b):
        there = (3 - j) % 3
        return pltpu.make_async_remote_copy(
            qbuf.at[6 + b], qbuf.at[3 * b + there], qsend.at[j, b], qrecv.at[there, b],
            device_id=dev(dx=SLOT_DX[j]), device_id_type=MESH,
        )

    def tcopy(j):
        there = (3 - j) % 3
        return pltpu.make_async_remote_copy(
            tbuf.at[3], tbuf.at[there], tsend.at[j], trecv.at[there], device_id=dev(dx=SLOT_DX[j]), device_id_type=MESH
        )

    send_own(0, 0)
    send_own(0, 1)
    node_in.wait()
    prepare_nodes((0, 1), (0,))
    send_own(1, 0)
    q_in.wait()
    for j in (1, 2, 0):
        for b in range(2):
            go(qcopy(j, b))
    for piece in range(4):
        go(ccopy(piece, 0))
    for copy in small_in:
        copy.wait()
    prepare_table()
    for j in range(3):
        go(tcopy(j))
    hop(0, 0, 1)
    hop(0, 1, 1)
    send_own(1, 1)
    prepare_nodes((), (1,))
    go(ccopy(4, 0))
    go(ccopy(5, 0))
    own_in.wait()
    prepare_own()
    hop(0, 0, 2)
    hop(0, 1, 2)
    send_own(2, 0)

    def queries_of(u, h):
        parts = [qbuf[u, :, h * 1024 + g * 128 : h * 1024 + g * 128 + 128] for g in range(GROUP)]
        return jnp.concatenate(parts, axis=0)

    def scores_of(keys, q):
        return lax.dot_general(keys, q, (((1,), (1,)), ((), ())), preferred_element_type=f32)

    def with_ones(vt):
        return jnp.concatenate([vt, jnp.ones((TAIL, vt.shape[1]), bf16)], axis=0)

    def clear(u, _):
        for h in range(2):
            acc[u, h] = jnp.zeros((DIM + TAIL, ROWS), f32)
            md[u, h] = jnp.full((8, ROWS), NEG, f32)
        return 0

    lax.fori_loop(0, 6, clear, 0)
    key_at = lax.broadcasted_iota(jnp.int32, (128, ROWS), 0)
    query_at = lax.rem(lax.broadcasted_iota(jnp.int32, (128, ROWS), 1), SEG)
    causal = key_at <= query_at
    for b in range(2):
        for h in range(2):
            s = scores_of(ownk[b, h], queries_of(6 + b, h))
            s = jnp.where(causal, s, NEG)
            m = jnp.max(s, axis=0, keepdims=True)
            p = jnp.exp2(s * C2 - m * C2).astype(bf16)
            acc[6 + b, h] = jnp.dot(with_ones(ownv[b, h]), p, preferred_element_type=f32)
            md[6 + b, h] = jnp.broadcast_to(m, (8, ROWS))

    hop(0, 0, 3)
    hop(0, 1, 3)
    send_own(2, 1)
    hop(1, 0, 1)
    hop(1, 1, 1)
    for j in range(3):
        tcopy((3 - j) % 3).wait_recv()
    t_in = local(9, tbuf, tsm)
    hop(0, 0, 4)
    hop(2, 0, 1)
    for j in range(3):
        for b in range(2):
            qcopy((3 - j) % 3, b).wait_recv()
    t_in.wait()
    settle(0, range(ZN))
    for h in range(2):
        for p in range(ZN):
            pair = jnp.concatenate([rv[p, 0, h], rv[p, 1, h]], axis=0).astype(f32)
            rvt[h, :, p * 128 : p * 128 + 128] = jnp.transpose(pair).astype(bf16)

    sbuf, rbuf = (s0, s1), (r0, r1)

    def unit_a(u, h, t, keys, biases):
        q = queries_of(u, h)
        old = md[u, h, 0:1, :]
        top = old
        for i in range(0, len(keys), 2):
            s = scores_of(jnp.concatenate(keys[i : i + 2], axis=0), q)
            sbuf[t][i * 128 : i * 128 + 256, :] = s
            for n in range(2):
                best = jnp.max(s[n * 128 : n * 128 + 128], axis=0, keepdims=True)
                top = jnp.maximum(top, best if biases is None else best + biases[i + n])
        md[u, h, 0:1, :] = top
        rbuf[t][0:1, :] = top * C2
        rbuf[t][1:2, :] = jnp.exp2((old - top) * C2)

    def unit_b(u, h, t, vts, biases):
        low, factor = rbuf[t][0:1, :], rbuf[t][1:2, :]
        weights = []
        for i in range(8):
            less = low if biases is None else low - biases[i]
            weights.append(jnp.exp2(sbuf[t][i * 128 : i * 128 + 128, :] * C2 - less).astype(bf16))
        p = jnp.concatenate(weights, axis=0)
        vt = vts[0] if len(vts) == 1 else jnp.concatenate(vts, axis=1)
        acc[u, h] = acc[u, h] * factor + jnp.dot(with_ones(vt), p, preferred_element_type=f32)

    def pipeline(unit_1, unit_2, after=None, hooks=()):
        unit_1(0, 0)

        def body(j, _):
            unit_1(2 * j + 1, 1)
            unit_2(2 * j, 0)
            if after is not None:
                after(2 * j)
            unit_1(2 * j + 2, 0)
            unit_2(2 * j + 1, 1)
            if after is not None:
                after(2 * j + 1)
            return 0

        at = 0
        for when, hook in hooks:
            lax.fori_loop(at, when, body, 0)
            hook()
            at = when
        lax.fori_loop(at, 3, body, 0)
        unit_1(7, 1)
        unit_2(6, 0)
        unit_2(7, 1)

    def root_stage(h, hooks=()):
        def first(u, t):
            unit_a(u, h, t, [jnp.concatenate([rk[p, 0, h], rk[p, 1, h]], axis=0) for p in range(ZN)], None)

        def second(u, t):
            unit_b(u, h, t, [rvt[h]], None)

        pipeline(first, second, None, hooks)

    def bias_of(active):
        return jnp.where(active, 0.0, NEG).astype(f32)

    def node_stage(h, after=None, hooks=()):
        def names(u):
            j, b = split(u)
            got, biases = [], []
            for l in range(8):
                code = tsm[j, b, l]
                owner = code >> 2
                at = ((owner >> 3) - z + ZN) & (ZN - 1)
                core = (owner + c) & 1
                mine = (code > 0) & (((owner >> 1) & (XN - 1)) == x)
                biases.append(bias_of(mine))
                got.append((at, core, jnp.clip((code & 3) - 1, 0, SLOTS - 1)))
            return got, biases

        def first(u, t):
            at, biases = names(u)
            unit_a(u, h, t, [nodes[h][0][a] for a in at], biases)

        def second(u, t):
            at, biases = names(u)
            unit_b(u, h, t, [nodes[h][1][a] for a in at], biases)

        pipeline(first, second, after, hooks)

    def three(v):
        a = v.astype(bf16).astype(f32)
        b = (v - a).astype(bf16).astype(f32)
        return [a, b, v - a - b]

    def ocopy(j, b, h):
        there = slot_there(j)
        return pltpu.make_async_remote_copy(
            sendbuf.at[h, j, b], recvbuf.at[h, there, b], osend.at[h, j, b], orecv.at[h, there, b],
            device_id=dev(dx=slot_dx(j)), device_id_type=MESH,
        )

    def send_part(h):
        def after(u):
            j, b = split(u)
            sendbuf[h, j, b, :DIM, :] = acc[u, h, :DIM, :].astype(bf16)
            tail = three(md[u, h, 0:1, :]) + three(acc[u, h, DIM : DIM + 1, :])
            tail = jnp.concatenate(tail + [jnp.zeros((TAIL - 6, ROWS), f32)], axis=0)
            sendbuf[h, j, b, DIM:, :] = tail.astype(bf16)
            ocopy(j, b, h).start()

        return after

    def merge(h):
        for b in range(2):
            for j in range(3):
                ocopy((3 - j) % 3, b, h).wait_recv()
            tops, dens, sums = [md[6 + b, h, 0:1, :]], [acc[6 + b, h, DIM : DIM + 1, :]], [acc[6 + b, h, :DIM, :]]
            for j in range(3):
                tail = recvbuf[h, j, b, DIM:, :].astype(f32)
                tops.append(tail[0:1] + tail[1:2] + tail[2:3])
                dens.append(tail[3:4] + tail[4:5] + tail[5:6])
                sums.append(recvbuf[h, j, b, :DIM, :].astype(f32))
            top = functools.reduce(jnp.maximum, tops)
            ws = [jnp.exp2((t - top) * C2) for t in tops]
            den = sum(w * d for w, d in zip(ws, dens))
            inv = 1.0 / den
            total = sum(s * (w * inv) for s, w in zip(sums, ws))
            live = lax.rem(lax.broadcasted_iota(jnp.int32, (1, ROWS), 1), SEG) < seg_s[b]
            total = jnp.where(live, total, 0.0)
            part = jnp.sum(total * total, axis=0, keepdims=True)
            ssq[b : b + 1, :] = part if h == 0 else ssq[b : b + 1, :] + part
            rows = jnp.transpose(total)
            for g in range(GROUP):
                at = h * 1024 + g * 128
                att[b, :, at : at + 128] = rows[g * SEG : g * SEG + SEG, :]

    root_stage(0)
    root_stage(1, [(1, lambda: hop(1, 0, 2)), (2, lambda: hop(1, 1, 2))])
    hop(1, 0, 3)
    hop(2, 1, 1)
    hop(2, 0, 2)
    hop(1, 1, 3)
    hop(1, 0, 4)
    hop(2, 1, 2)
    settle(1, range(ZN))
    node_stage(0, send_part(0), [(2, lambda: hop(2, 0, 3))])
    hop(2, 1, 3)
    hop(2, 0, 4)
    settle(2, range(ZN))
    node_stage(1, send_part(1))
    merge(0)
    merge(1)

    def ycopy(d):
        return pltpu.make_async_remote_copy(
            ssq, ssq_in.at[3 - d], ysend.at[d - 1], yrecv.at[3 - d], device_id=dev(dy=d), device_id_type=MESH
        )

    for d in (1, 2, 3):
        go(ycopy(d))
    for d in (1, 2, 3):
        ycopy(d).wait_recv()
    gain_in.wait()
    squares = jnp.transpose(ssq[...] + ssq_in[0] + ssq_in[1] + ssq_in[2])
    squares = sum(squares[g * SEG : g * SEG + SEG, :] for g in range(GROUP))
    scales = lax.rsqrt(squares / (HEADS * DIM) + 1e-6)
    for b in range(2):
        scale = scales[:, b : b + 1]
        for g in range(2 * GROUP):
            at = slice(g * 128, g * 128 + 128)
            out_ref[b, :, at] = (att[b, :, at] * scale * gain_ref[at].astype(f32).reshape(1, DIM)).astype(bf16)

    for copy in started:
        copy.wait_send()
    for h in range(2):
        for j in range(3):
            for b in range(2):
                ocopy(j, b, h).wait_send()


def on_device(queries, root_kv, node_kv, own_kv, anc_owner, anc_slot, depth_len, seg_len, norm_gain):
    bf16, f32 = jnp.bfloat16, jnp.float32

    def rows_of(kv):
        lead = kv.shape[:-2]
        n = len(lead)
        kv = kv.reshape(lead + (2, 2, DIM))
        kv = kv.transpose(tuple(range(n)) + (n + 1, n, n + 2))
        return kv.reshape(-1, DIM)

    node_refs = [pltpu.VMEM((ZN, 2, SLOTS, 128, 128), bf16) for _ in range(4)]
    dma = pltpu.SemaphoreType.DMA
    scratch = [
        pltpu.VMEM((2 * 2 * ROOT, DIM), bf16),
        pltpu.VMEM((SLOTS * 2 * 2 * 128, DIM), bf16),
        pltpu.VMEM((2 * 2 * 2 * SEG, DIM), bf16),
        pltpu.SMEM((2, 8), jnp.int32),
        pltpu.SMEM((2, 8), jnp.int32),
        pltpu.SMEM((2,), jnp.int32),
        pltpu.SMEM((2,), jnp.int32),
        pltpu.VMEM((2048,), bf16),
        pltpu.VMEM((2 * XN, SEG, 2048), bf16),
        pltpu.VMEM((ZN, 2, 2, ROOT, DIM), bf16),
        pltpu.VMEM((ZN, 2, 2, ROOT, DIM), bf16),
        pltpu.VMEM((2, DIM, ZN * 2 * ROOT), bf16),
        pltpu.VMEM((2, 2, 128, DIM), bf16),
        pltpu.VMEM((2, 2, DIM, 128), bf16),
        *node_refs,
        pltpu.VMEM((8, 2, DIM + TAIL, ROWS), f32),
        pltpu.VMEM((8, 2, 8, ROWS), f32),
        pltpu.VMEM((1024, ROWS), f32),
        pltpu.VMEM((1024, ROWS), f32),
        pltpu.VMEM((8, ROWS), f32),
        pltpu.VMEM((8, ROWS), f32),
        pltpu.VMEM((XN, 8, 128), jnp.int32),
        pltpu.SMEM((XN, 8, 128), jnp.int32),
        pltpu.VMEM((2, 3, 2, DIM + TAIL, ROWS), bf16),
        pltpu.VMEM((2, 3, 2, DIM + TAIL, ROWS), bf16),
        pltpu.VMEM((2, SEG, 2048), f32),
        pltpu.VMEM((8, ROWS), f32),
        pltpu.VMEM((3, 8, ROWS), f32),
        dma((NPIECE, 2, 4)),
        dma((NPIECE, 2, 4)),
        dma((NPIECE, 8)),
        dma((NPIECE, 8)),
        dma((3, 2)),
        dma((3, 2)),
        dma((3,)),
        dma((3,)),
        dma((2, 3, 2)),
        dma((2, 3, 2)),
        dma((3,)),
        dma((3,)),
        dma((10,)),
    ]
    return pl.pallas_call(
        kernel,
        out_shape=jax.ShapeDtypeStruct(queries.shape, bf16),
        in_specs=[pl.BlockSpec(memory_space=pltpu.HBM)] * 9,
        out_specs=pl.BlockSpec(memory_space=pltpu.VMEM),
        scratch_shapes=scratch,
        compiler_params=pltpu.CompilerParams(
            collective_id=0, has_side_effects=True, vmem_limit_bytes=48 * 2**20
        ),
        name="tree_attention",
    )(
        *[
            pltpu.with_memory_space_constraint(v, pltpu.HBM)
            for v in (
                queries, rows_of(root_kv), rows_of(node_kv), rows_of(own_kv),
                anc_owner, anc_slot, depth_len, seg_len, norm_gain,
            )
        ]
    )


def solution(mesh):
    in_specs = (
        P("branch", None, "blk"),
        P("branch", None, "blk"),
        P("branch", None, None, "blk"),
        P("branch", None, None, "blk"),
        P("branch", None),
        P("branch", None),
        P("branch"),
        P("branch"),
        P("blk"),
    )
    return jax.shard_map(
        on_device, mesh=mesh, in_specs=in_specs, out_specs=P("branch", None, "blk"), check_vma=False
    )
```

```python
import functools
import math

import jax
import jax.numpy as jnp
from jax import lax
from jax.experimental import pallas as pl
from jax.experimental.pallas import tpu as pltpu
from jax.sharding import PartitionSpec as P

MESH = pl.DeviceIdType.MESH
HEADS = 64
DIM = 128
SEG = 32
GROUP = 8
SLOTS = 3
ROWS = GROUP * SEG
ROOT = 64
ZN = 8
XN = 4
C2 = math.log2(math.e) / math.sqrt(DIM)
NEG = -1e30
TAIL = 16
POS_DZ = (0, -1, 1, -2, 2, -3, 3, 4)
SLOT_DX = (2, 1, 3)
NRING = 6


def pos_of(step, direction):
    return 7 if step == 4 else 2 * step - 1 + direction


def kernel(
    q_hbm, root_hbm, node_hbm, own_hbm, owner_hbm, slot_hbm, depth_hbm, seg_hbm, gain_hbm, out_ref,
    root_x, node_x, own_x, owner_s, slot_s, depth_s, seg_s, gain_ref,
    qb0, qb1, rk0, rv0, rvt0, rk1, rv1, rvt1, ownk, ownv, k0, v0, k1, v1,
    acc0, acc1, md0, md1, s0, s1, r0, r1, tx, tz, txs, tzs, send0, recv0, send1, recv1, att, ssq, ssq_in,
    zsend, zrecv, csend, crecv, xsend, xrecv, dsend, drecv, qsend, qrecv, tsend, trecv, usend, urecv,
    osend, orecv, psend, precv, ysend, yrecv, lsem,
):
    bf16, f32 = jnp.bfloat16, jnp.float32
    y = lax.axis_index("blk")
    r = lax.axis_index("branch")
    z, x, c = r // 8, (r // 2) % 4, r % 2

    def dev(dy=0, dz=0, dx=0, dc=0):
        zz = lax.rem(z + dz + ZN, ZN)
        xx = lax.rem(x + dx + XN, XN)
        cc = lax.rem(c + dc, 2)
        return (lax.rem(y + dy, 4), zz * 8 + xx * 2 + cc)

    def remote(src, dst, ssem, rsem, to):
        return pltpu.make_async_remote_copy(src, dst, ssem, rsem, device_id=to, device_id_type=MESH)

    bar = pltpu.get_barrier_semaphore()
    up, down, other = dev(dz=1), dev(dz=-1), dev(dc=1)
    peers = [other] + [dev(dz=d) for d in range(1, 8)]
    peers += [dev(dx=d) for d in (1, 2, 3)] + [dev(dy=d) for d in (1, 2, 3)]
    for p in peers:
        pl.semaphore_signal(bar, inc=1, device_id=p, device_id_type=MESH)

    def local(i, src, dst):
        copy = pltpu.make_async_copy(src, dst, lsem.at[i])
        copy.start()
        return copy

    root_in = local(1, root_hbm, root_x)
    node_in = local(0, node_hbm, node_x)
    small_in = [
        local(2, owner_hbm, owner_s), local(3, slot_hbm, slot_s), local(4, depth_hbm, depth_s), local(5, seg_hbm, seg_s)
    ]
    q_in = [
        local(6, q_hbm.at[:, :, pl.ds(0, 1024)], qb0.at[pl.ds(6, 2)]),
        local(9, q_hbm.at[:, :, pl.ds(1024, 1024)], qb1.at[pl.ds(0, 2)]),
    ]
    own_in = local(7, own_hbm, own_x)
    gain_in = local(8, gain_hbm, gain_ref)

    row = lax.broadcasted_iota(jnp.int32, (128, 128), 0)
    col = lax.broadcasted_iota(jnp.int32, (128, 128), 1)
    want = (row % 32) * 4 + row // 32
    pick = jnp.where(col == want, 1.0, 0.0).astype(bf16)

    def apart(ref, first):
        return jnp.dot(pick, ref[first : first + 128, :], preferred_element_type=f32)

    def prepare_root():
        got = [apart(root_x, t * 128).astype(bf16) for t in range(2)]
        for h, (kr, vr) in enumerate(((rk0, rv0), (rk1, rv1))):
            for t in range(2):
                kr[0, 0, t * 32 : t * 32 + 32, :] = got[t][h * 64 : h * 64 + 32]
                vr[0, 0, t * 32 : t * 32 + 32, :] = got[t][h * 64 + 32 : h * 64 + 64]

    def prepare_nodes(h, kr, vr):
        for s in range(SLOTS):
            got = [apart(node_x, (s * 4 + t) * 128) for t in range(4)]
            keys = jnp.concatenate([g[h * 64 : h * 64 + 32] for g in got], axis=0)
            vals = jnp.concatenate([g[h * 64 + 32 : h * 64 + 64] for g in got], axis=0)
            kr[0, 0, s] = keys.astype(bf16)
            vr[0, 0, s] = jnp.transpose(vals).astype(bf16)

    def prepare_own():
        zeros96 = jnp.zeros((96, 128), f32)
        for b in range(2):
            got = apart(own_x, b * 128)
            for h in range(2):
                keys = jnp.concatenate([got[h * 64 : h * 64 + 32], zeros96], axis=0)
                vals = jnp.concatenate([got[h * 64 + 32 : h * 64 + 64], zeros96], axis=0)
                ownk[b, h] = keys.astype(bf16)
                ownv[b, h] = jnp.transpose(vals).astype(bf16)

    def prepare_table():
        lane = lax.broadcasted_iota(jnp.int32, (8, 128), 1)
        sub = lax.broadcasted_iota(jnp.int32, (8, 128), 0)
        table = jnp.zeros((8, 128), jnp.int32)
        for b in range(2):
            for l in range(8):
                code = jnp.where(l < depth_s[b], 4 * owner_s[b, l] + slot_s[b, l] + 1, 0)
                table = jnp.where((lane == l) & (sub == b), code, table)
        tx[3] = table
        tz[0] = table

    root_in.wait()
    prepare_root()
    pl.semaphore_wait(bar, len(peers))

    started = []

    def go(copy):
        copy.start()
        started.append(copy)

    def view(piece, pos, core):
        dz = POS_DZ[pos] % ZN
        if piece < 2:
            return qb1.at[2 * dz + piece]
        return (k0, v0, rk0, rv0)[piece - 2].at[dz, core]

    def zcopy(piece, direction, step):
        if step > 1:
            src = view(piece, pos_of(step - 1, direction), 0)
        elif piece < 2:
            src = q_hbm.at[piece, :, pl.ds(1024, 1024)]
        else:
            src = view(piece, 0, 0)
        return remote(
            src, view(piece, pos_of(step, direction), 0), zsend.at[piece, direction, step - 1],
            zrecv.at[piece, direction, step - 1], up if direction == 0 else down,
        )

    def ccopy(piece, pos):
        return remote(view(piece, pos, 0), view(piece, pos, 1), csend.at[piece, pos], crecv.at[piece, pos], other)

    def send_own(kind, which):
        for direction in (0, 1):
            go(zcopy(2 * kind + (which ^ direction), direction, 1))

    def hop(kind, which, step):
        for direction in (0, 1):
            piece = 2 * kind + (which ^ direction)
            zcopy(piece, direction, step).wait_recv()
            if step < 3 or (step == 3 and which == 0):
                go(zcopy(piece, direction, step + 1))
            if kind > 0:
                go(ccopy(piece, pos_of(step, direction)))

    def settle(kind):
        for pos in range(ZN):
            for piece in (2 * kind, 2 * kind + 1):
                ccopy(piece, pos).wait_recv()

    xrefs = (k1, v1, rk1, rv1)

    def xcopy(piece, dx):
        there = 4 - dx
        return remote(
            xrefs[piece].at[0, 0], xrefs[piece].at[there, 0], xsend.at[piece, dx - 1], xrecv.at[piece, there - 1], dev(dx=dx)
        )

    def dcopy(piece, rel):
        ref = xrefs[piece]
        return remote(ref.at[rel, 0], ref.at[rel, 1], dsend.at[piece, rel], drecv.at[piece, rel], other)

    def slot_dx(j):
        return jnp.where(j == 0, 2, 2 * j - 1)

    def slot_there(j):
        return lax.rem(3 - j, 3)

    def split(u):
        return jnp.where(u < 6, lax.rem(u, 3), 3), jnp.where(u < 6, lax.div(u, 3), u - 6)

    def qcopy(j, b):
        there = (3 - j) % 3
        return remote(
            q_hbm.at[b, :, pl.ds(0, 1024)], qb0.at[3 * b + there], qsend.at[j, b], qrecv.at[there, b], dev(dx=SLOT_DX[j])
        )

    def tcopy(j):
        there = (3 - j) % 3
        return remote(tx.at[3], tx.at[there], tsend.at[j], trecv.at[there], dev(dx=SLOT_DX[j]))

    def ucopy(dz):
        return remote(tz.at[0], tz.at[8 - dz], usend.at[dz - 1], urecv.at[7 - dz], dev(dz=dz))

    send_own(0, 0)
    send_own(0, 1)
    send_own(2, 0)
    send_own(2, 1)
    node_in.wait()
    prepare_nodes(1, k1, v1)
    for piece in (0, 1):
        for dx in (1, 3, 2):
            go(xcopy(piece, dx))
    hop(0, 0, 1)
    hop(0, 1, 1)
    prepare_nodes(0, k0, v0)
    send_own(1, 0)
    for piece in (2, 3):
        for dx in (1, 3, 2):
            go(xcopy(piece, dx))
    for copy in small_in:
        copy.wait()
    prepare_table()
    for dz in range(1, 8):
        go(ucopy(dz))
    hop(0, 0, 2)
    hop(0, 1, 2)
    for j in range(3):
        go(tcopy(j))
    for b in range(2):
        for j in (1, 2, 0):
            go(qcopy(j, b))
    for piece in range(4):
        go(dcopy(piece, 0))
        go(ccopy(2 + piece, 0))
    own_in.wait()
    prepare_own()
    hop(0, 0, 3)
    send_own(1, 1)
    hop(2, 0, 1)
    hop(2, 1, 1)
    hop(1, 0, 1)
    for copy in q_in:
        copy.wait()

    qbs, accs, mds = (qb0, qb1), (acc0, acc1), (md0, md1)

    def queries_of(u, h):
        return jnp.concatenate([qbs[h][u, :, g * 128 : g * 128 + 128] for g in range(GROUP)], axis=0)

    def scores_of(keys, q):
        return lax.dot_general(keys, q, (((1,), (1,)), ((), ())), preferred_element_type=f32)

    def with_ones(vt):
        return jnp.concatenate([vt, jnp.ones((TAIL, vt.shape[1]), bf16)], axis=0)

    def clear(h):
        def body(u, _):
            accs[h][u] = jnp.zeros((DIM + TAIL, ROWS), f32)
            mds[h][u] = jnp.full((8, ROWS), NEG, f32)
            return 0

        return body

    lax.fori_loop(0, 6, clear(0), 0)
    lax.fori_loop(2, 16, clear(1), 0)
    for piece in (0, 1, 2, 3):
        for dx in (1, 3, 2):
            xcopy(piece, dx).wait_recv()
            go(dcopy(piece, 4 - dx))
    hop(0, 1, 3)
    key_at = lax.broadcasted_iota(jnp.int32, (128, ROWS), 0)
    query_at = lax.rem(lax.broadcasted_iota(jnp.int32, (128, ROWS), 1), SEG)
    causal = key_at <= query_at
    for b in range(2):
        for h in range(2):
            u = (6 + b, b)[h]
            s = scores_of(ownk[b, h], queries_of(u, h))
            s = jnp.where(causal, s, NEG)
            m = jnp.max(s, axis=0, keepdims=True)
            p = jnp.exp2(s * C2 - m * C2).astype(bf16)
            accs[h][u] = jnp.dot(with_ones(ownv[b, h]), p, preferred_element_type=f32)
            mds[h][u] = jnp.broadcast_to(m, (8, ROWS))
    for dz in range(1, 8):
        ucopy(dz).wait_recv()
    for j in range(3):
        tcopy((3 - j) % 3).wait_recv()
    t_in = [local(10, tx, txs), local(11, tz, tzs)]
    hop(0, 0, 4)
    for copy in t_in:
        copy.wait()
    for piece in range(4):
        for rel in range(4):
            dcopy(piece, rel).wait_recv()

    def turn(vr, vt, n):
        for p in range(n):
            pair = jnp.concatenate([vr[p, 0], vr[p, 1]], axis=0).astype(f32)
            vt[p] = jnp.transpose(pair).astype(bf16)

    turn(rv1, rvt1, 4)

    sbuf, rbuf = (s0, s1), (r0, r1)

    def unit_a(u, h, t, keys, biases):
        q = queries_of(u, h)
        old = mds[h][u, 0:1, :]
        top = old
        for i in range(0, len(keys), 2):
            s = scores_of(jnp.concatenate(keys[i : i + 2], axis=0), q)
            sbuf[t][i * 128 : i * 128 + 256, :] = s
            for n in range(2):
                best = jnp.max(s[n * 128 : n * 128 + 128], axis=0, keepdims=True)
                top = jnp.maximum(top, best if biases[i + n] is None else best + biases[i + n])
        mds[h][u, 0:1, :] = top
        rbuf[t][0:1, :] = top * C2
        rbuf[t][1:2, :] = jnp.exp2((old - top) * C2)

    def unit_b(u, h, t, vts, biases):
        low, factor = rbuf[t][0:1, :], rbuf[t][1:2, :]
        weights = []
        for i, bias in enumerate(biases):
            less = low if bias is None else low - bias
            weights.append(jnp.exp2(sbuf[t][i * 128 : i * 128 + 128, :] * C2 - less).astype(bf16))
        p = jnp.concatenate(weights, axis=0)
        vt = jnp.concatenate(vts, axis=1)
        accs[h][u] = accs[h][u] * factor + jnp.dot(with_ones(vt), p, preferred_element_type=f32)

    def pipeline(count, unit_1, unit_2, after=None, hooks=()):
        unit_1(0, 0)

        def body(j, _):
            unit_1(2 * j + 1, 1)
            unit_2(2 * j, 0)
            if after is not None:
                after(2 * j)
            unit_1(2 * j + 2, 0)
            unit_2(2 * j + 1, 1)
            if after is not None:
                after(2 * j + 1)
            return 0

        at = 0
        for when, hook in hooks:
            lax.fori_loop(at, when, body, 0)
            hook()
            at = when
        lax.fori_loop(at, count // 2 - 1, body, 0)
        unit_1(count - 1, 1)
        unit_2(count - 2, 0)
        unit_2(count - 1, 1)

    def bias_of(active):
        return jnp.where(active, 0.0, NEG).astype(f32)

    def pairs(ref, n):
        return [jnp.concatenate([ref[p, 0], ref[p, 1]], axis=0) for p in range(n)]

    def slot_of(code):
        return jnp.clip((code & 3) - 1, 0, SLOTS - 1)

    def column_stage(after, hooks=()):
        def names(u):
            j, b = split(u)
            got, biases = [], [None] * ZN
            for l in range(8):
                code = txs[j, b, l]
                owner = code >> 2
                biases.append(bias_of((code > 0) & (((owner >> 1) & (XN - 1)) == x)))
                got.append((((owner >> 3) - z + ZN) & (ZN - 1), (owner + c) & 1, slot_of(code)))
            return got, biases

        def first(u, t):
            at, biases = names(u)
            unit_a(u, 0, t, pairs(rk0, ZN) + [k0[a] for a in at], biases)

        def second(u, t):
            at, biases = names(u)
            unit_b(u, 0, t, [rvt0[p] for p in range(ZN)] + [v0[a] for a in at], biases)

        pipeline(8, first, second, after, hooks)

    def row_stage(hooks=()):
        def names(u):
            got, biases = [], [None] * XN
            for l in range(8):
                code = tzs[u // 2, u % 2, l]
                owner = code >> 2
                biases.append(bias_of((code > 0) & ((owner >> 3) == z)))
                got.append((((owner >> 1) - x + XN) & (XN - 1), (owner + c) & 1, slot_of(code)))
            return got, biases

        def first(u, t):
            at, biases = names(u)
            unit_a(u, 1, t, pairs(rk1, XN) + [k1[a] for a in at], biases)

        def second(u, t):
            at, biases = names(u)
            unit_b(u, 1, t, [rvt1[p] for p in range(XN)] + [v1[a] for a in at], biases)

        pipeline(16, first, second, None, hooks)

    def three(v):
        a = v.astype(bf16).astype(f32)
        b = (v - a).astype(bf16).astype(f32)
        return [a, b, v - a - b]

    def write(ref, total, top, den):
        ref[:DIM, :] = total.astype(bf16)
        tail = jnp.concatenate(three(top) + three(den) + [jnp.zeros((TAIL - 6, ROWS), f32)], axis=0)
        ref[DIM:, :] = tail.astype(bf16)

    def read(ref):
        tail = ref[DIM:, :].astype(f32)
        return ref[:DIM, :].astype(f32), tail[0:1] + tail[1:2] + tail[2:3], tail[3:4] + tail[4:5] + tail[5:6]

    def state(h, u):
        return accs[h][u, :DIM, :], mds[h][u, 0:1, :], accs[h][u, DIM : DIM + 1, :]

    def combine(parts):
        top = functools.reduce(jnp.maximum, [p[1] for p in parts])
        ws = [jnp.exp2((p[1] - top) * C2) for p in parts]
        return ws, top, sum(w * p[2] for w, p in zip(ws, parts))

    def ocopy(j, b):
        there = slot_there(j)
        return remote(send0.at[j, b], recv0.at[there, b], osend.at[j, b], orecv.at[there, b], dev(dx=slot_dx(j)))

    def send_part(u):
        j, b = split(u)
        write(send0.at[j, b], *state(0, u))
        ocopy(j, b).start()

    def pcopy(direction, step, b):
        return remote(
            send1.at[direction, step - 1, b], recv1.at[direction, step - 1, b], psend.at[direction, step - 1, b],
            precv.at[direction, step - 1, b], up if direction == 0 else down,
        )

    def pass_on(step, fresh):
        for direction in (0, 1):
            b = direction ^ fresh
            away = 5 - step if direction == 0 else 3 + step
            mine = state(1, 2 * away + b)
            if step > 2 or (step == 2 and fresh == 0):
                pcopy(direction, step - 1, b).wait_recv()
                parts = [mine, read(recv1.at[direction, step - 2, b])]
                ws, top, den = combine(parts)
                mine = (sum(w * p[0] for w, p in zip(ws, parts)), top, den)
            write(send1.at[direction, step - 1, b], *mine)
            go(pcopy(direction, step, b))

    def finish(h, b, u, parts):
        ws, top, den = combine(parts)
        inv = 1.0 / den
        total = sum(p[0] * (w * inv) for w, p in zip(ws, parts))
        live = lax.rem(lax.broadcasted_iota(jnp.int32, (1, ROWS), 1), SEG) < seg_s[b]
        total = jnp.where(live, total, 0.0)
        part = jnp.sum(total * total, axis=0, keepdims=True)
        ssq[b : b + 1, :] = part if h == 0 else ssq[b : b + 1, :] + part
        rows = jnp.transpose(total)
        for g in range(GROUP):
            at = h * 1024 + g * 128
            att[b, :, at : at + 128] = rows[g * SEG : g * SEG + SEG, :]

    def merge0(b):
        for j in range(3):
            ocopy((3 - j) % 3, b).wait_recv()
        finish(0, b, 6 + b, [state(0, 6 + b)] + [read(recv0.at[j, b]) for j in range(3)])

    def merge1(b):
        for direction in (0, 1):
            pcopy(direction, 4, b).wait_recv()
        finish(1, b, b, [state(1, b)] + [read(recv1.at[direction, 3, b]) for direction in (0, 1)])

    def hook_root():
        hop(2, 0, 2)
        hop(2, 1, 2)

    row_stage([(2, lambda: hop(1, 1, 1)), (3, hook_root), (5, lambda: hop(1, 0, 2))])
    hop(1, 1, 2)
    hop(2, 0, 3)
    hop(2, 1, 3)
    hop(1, 0, 3)
    pass_on(1, 0)
    pass_on(2, 1)
    hop(1, 1, 3)
    for j in range(3):
        for b in range(2):
            qcopy((3 - j) % 3, b).wait_recv()
    hop(2, 0, 4)
    settle(2)
    turn(rv0, rvt0, ZN)
    hop(1, 0, 4)
    pass_on(2, 0)
    settle(1)
    column_stage(send_part, [(1, lambda: pass_on(3, 1)), (2, lambda: pass_on(3, 0)), (3, lambda: pass_on(4, 1))])
    pass_on(4, 0)
    merge0(0)
    merge0(1)
    merge1(0)
    merge1(1)

    def ycopy(d):
        return pltpu.make_async_remote_copy(
            ssq, ssq_in.at[3 - d], ysend.at[d - 1], yrecv.at[3 - d], device_id=dev(dy=d), device_id_type=MESH
        )

    for d in (1, 2, 3):
        go(ycopy(d))
    for d in (1, 2, 3):
        ycopy(d).wait_recv()
    gain_in.wait()
    squares = jnp.transpose(ssq[...] + ssq_in[0] + ssq_in[1] + ssq_in[2])
    squares = sum(squares[g * SEG : g * SEG + SEG, :] for g in range(GROUP))
    scales = lax.rsqrt(squares / (HEADS * DIM) + 1e-6)
    for b in range(2):
        scale = scales[:, b : b + 1]
        for g in range(2 * GROUP):
            at = slice(g * 128, g * 128 + 128)
            out_ref[b, :, at] = (att[b, :, at] * scale * gain_ref[at].astype(f32).reshape(1, DIM)).astype(bf16)

    for copy in started:
        copy.wait_send()
    for j in range(3):
        for b in range(2):
            ocopy(j, b).wait_send()


def on_device(queries, root_kv, node_kv, own_kv, anc_owner, anc_slot, depth_len, seg_len, norm_gain):
    bf16, f32 = jnp.bfloat16, jnp.float32

    def rows_of(kv):
        lead = kv.shape[:-2]
        n = len(lead)
        kv = kv.reshape(lead + (2, 2, DIM))
        kv = kv.transpose(tuple(range(n)) + (n + 1, n, n + 2))
        return kv.reshape(-1, DIM)

    dma = pltpu.SemaphoreType.DMA
    scratch = [
        pltpu.VMEM((2 * 2 * ROOT, DIM), bf16),
        pltpu.VMEM((SLOTS * 2 * 2 * 128, DIM), bf16),
        pltpu.VMEM((2 * 2 * 2 * SEG, DIM), bf16),
        pltpu.SMEM((2, 8), jnp.int32),
        pltpu.SMEM((2, 8), jnp.int32),
        pltpu.SMEM((2,), jnp.int32),
        pltpu.SMEM((2,), jnp.int32),
        pltpu.VMEM((2048,), bf16),
        pltpu.VMEM((8, SEG, 1024), bf16),
        pltpu.VMEM((16, SEG, 1024), bf16),
        pltpu.VMEM((ZN, 2, ROOT, DIM), bf16),
        pltpu.VMEM((ZN, 2, ROOT, DIM), bf16),
        pltpu.VMEM((ZN, DIM, 2 * ROOT), bf16),
        pltpu.VMEM((XN, 2, ROOT, DIM), bf16),
        pltpu.VMEM((XN, 2, ROOT, DIM), bf16),
        pltpu.VMEM((XN, DIM, 2 * ROOT), bf16),
        pltpu.VMEM((2, 2, 128, DIM), bf16),
        pltpu.VMEM((2, 2, DIM, 128), bf16),
        pltpu.VMEM((ZN, 2, SLOTS, 128, DIM), bf16),
        pltpu.VMEM((ZN, 2, SLOTS, DIM, 128), bf16),
        pltpu.VMEM((XN, 2, SLOTS, 128, DIM), bf16),
        pltpu.VMEM((XN, 2, SLOTS, DIM, 128), bf16),
        pltpu.VMEM((8, DIM + TAIL, ROWS), f32),
        pltpu.VMEM((16, DIM + TAIL, ROWS), f32),
        pltpu.VMEM((8, 8, ROWS), f32),
        pltpu.VMEM((16, 8, ROWS), f32),
        pltpu.VMEM((2048, ROWS), f32),
        pltpu.VMEM((2048, ROWS), f32),
        pltpu.VMEM((8, ROWS), f32),
        pltpu.VMEM((8, ROWS), f32),
        pltpu.VMEM((XN, 8, 128), jnp.int32),
        pltpu.VMEM((ZN, 8, 128), jnp.int32),
        pltpu.SMEM((XN, 8, 128), jnp.int32),
        pltpu.SMEM((ZN, 8, 128), jnp.int32),
        pltpu.VMEM((3, 2, DIM + TAIL, ROWS), bf16),
        pltpu.VMEM((3, 2, DIM + TAIL, ROWS), bf16),
        pltpu.VMEM((2, 4, 2, DIM + TAIL, ROWS), bf16),
        pltpu.VMEM((2, 4, 2, DIM + TAIL, ROWS), bf16),
        pltpu.VMEM((2, SEG, 2048), f32),
        pltpu.VMEM((8, ROWS), f32),
        pltpu.VMEM((3, 8, ROWS), f32),
    ]
    for shape in ((NRING, 2, 4), (NRING, 8), (4, 3), (4, 4), (3, 2), (3,), (7,), (3, 2), (2, 4, 2), (3,)):
        scratch += [dma(shape), dma(shape)]
    scratch.append(dma((12,)))
    return pl.pallas_call(
        kernel,
        out_shape=jax.ShapeDtypeStruct(queries.shape, bf16),
        in_specs=[pl.BlockSpec(memory_space=pltpu.HBM)] * 9,
        out_specs=pl.BlockSpec(memory_space=pltpu.VMEM),
        scratch_shapes=scratch,
        compiler_params=pltpu.CompilerParams(
            collective_id=0, has_side_effects=True, vmem_limit_bytes=48 * 2**20
        ),
        name="tree_attention",
    )(
        *[
            pltpu.with_memory_space_constraint(v, pltpu.HBM)
            for v in (
                queries, rows_of(root_kv), rows_of(node_kv), rows_of(own_kv),
                anc_owner, anc_slot, depth_len, seg_len, norm_gain,
            )
        ]
    )


def solution(mesh):
    in_specs = (
        P("branch", None, "blk"),
        P("branch", None, "blk"),
        P("branch", None, None, "blk"),
        P("branch", None, None, "blk"),
        P("branch", None),
        P("branch", None),
        P("branch"),
        P("branch"),
        P("blk"),
    )
    return jax.shard_map(
        on_device, mesh=mesh, in_specs=in_specs, out_specs=P("branch", None, "blk"), check_vma=False
    )
```

```python
import functools
import math

import jax
import jax.numpy as jnp
from jax import lax
from jax.experimental import pallas as pl
from jax.experimental.pallas import tpu as pltpu
from jax.sharding import PartitionSpec as P

MESH = pl.DeviceIdType.MESH
HEADS = 64
DIM = 128
SEG = 32
GROUP = 8
SLOTS = 3
ROWS = GROUP * SEG
ROOT = 64
ZN = 8
XN = 4
C2 = math.log2(math.e) / math.sqrt(DIM)
NEG = -1e30
TAIL = 16
POS_DZ = (0, -1, 1, -2, 2, -3, 3, 4)
SLOT_DX = (2, 1, 3)
NRING = 6


def pos_of(step, direction):
    return 7 if step == 4 else 2 * step - 1 + direction


def kernel(
    q_hbm, root_hbm, node_hbm, own_hbm, owner_hbm, slot_hbm, depth_hbm, seg_hbm, gain_hbm, out_ref,
    root_x, node_x, own_x, owner_s, slot_s, depth_s, seg_s, gain_ref,
    qb0, qb1, rk0, rv0, rvt0, rk1, rv1, rvt1, ownk, ownv, k0, v0, k1, v1,
    acc0, acc1, md0, md1, s0, s1, r0, r1, tx, tz, txs, tzs, send0, recv0, send1, recv1, att, ssq, ssq_in,
    zsend, zrecv, csend, crecv, xsend, xrecv, dsend, drecv, qsend, qrecv, tsend, trecv, usend, urecv,
    osend, orecv, psend, precv, ysend, yrecv, lsem,
):
    bf16, f32 = jnp.bfloat16, jnp.float32
    y = lax.axis_index("blk")
    r = lax.axis_index("branch")
    z, x, c = r // 8, (r // 2) % 4, r % 2

    def dev(dy=0, dz=0, dx=0, dc=0):
        zz = lax.rem(z + dz + ZN, ZN)
        xx = lax.rem(x + dx + XN, XN)
        cc = lax.rem(c + dc, 2)
        return (lax.rem(y + dy, 4), zz * 8 + xx * 2 + cc)

    def remote(src, dst, ssem, rsem, to):
        return pltpu.make_async_remote_copy(src, dst, ssem, rsem, device_id=to, device_id_type=MESH)

    bar = pltpu.get_barrier_semaphore()
    up, down, other = dev(dz=1), dev(dz=-1), dev(dc=1)
    peers = [other] + [dev(dz=d) for d in range(1, 8)]
    peers += [dev(dx=d) for d in (1, 2, 3)] + [dev(dy=d) for d in (1, 2, 3)]
    for p in peers:
        pl.semaphore_signal(bar, inc=1, device_id=p, device_id_type=MESH)

    def local(i, src, dst):
        copy = pltpu.make_async_copy(src, dst, lsem.at[i])
        copy.start()
        return copy

    root_in = local(1, root_hbm, root_x)
    node_in = local(0, node_hbm, node_x)
    small_in = [
        local(2, owner_hbm, owner_s), local(3, slot_hbm, slot_s), local(4, depth_hbm, depth_s), local(5, seg_hbm, seg_s)
    ]
    q_in = [
        local(6, q_hbm.at[:, :, pl.ds(0, 1024)], qb0.at[pl.ds(6, 2)]),
        local(9, q_hbm.at[:, :, pl.ds(1024, 1024)], qb1.at[pl.ds(0, 2)]),
    ]
    own_in = local(7, own_hbm, own_x)
    gain_in = local(8, gain_hbm, gain_ref)

    row = lax.broadcasted_iota(jnp.int32, (128, 128), 0)
    col = lax.broadcasted_iota(jnp.int32, (128, 128), 1)
    want = (row % 32) * 4 + row // 32
    pick = jnp.where(col == want, 1.0, 0.0).astype(bf16)

    def apart(ref, first):
        return jnp.dot(pick, ref[first : first + 128, :], preferred_element_type=f32)

    def prepare_root():
        got = [apart(root_x, t * 128).astype(bf16) for t in range(2)]
        for h, (kr, vr) in enumerate(((rk0, rv0), (rk1, rv1))):
            for t in range(2):
                kr[0, 0, t * 32 : t * 32 + 32, :] = got[t][h * 64 : h * 64 + 32]
                vr[0, 0, t * 32 : t * 32 + 32, :] = got[t][h * 64 + 32 : h * 64 + 64]

    def prepare_nodes(h, kr, vr):
        for s in range(SLOTS):
            got = [apart(node_x, (s * 4 + t) * 128) for t in range(4)]
            keys = jnp.concatenate([g[h * 64 : h * 64 + 32] for g in got], axis=0)
            vals = jnp.concatenate([g[h * 64 + 32 : h * 64 + 64] for g in got], axis=0)
            kr[0, 0, s] = keys.astype(bf16)
            vr[0, 0, s] = jnp.transpose(vals).astype(bf16)

    def prepare_own():
        zeros96 = jnp.zeros((96, 128), f32)
        for b in range(2):
            got = apart(own_x, b * 128)
            for h in range(2):
                keys = jnp.concatenate([got[h * 64 : h * 64 + 32], zeros96], axis=0)
                vals = jnp.concatenate([got[h * 64 + 32 : h * 64 + 64], zeros96], axis=0)
                ownk[b, h] = keys.astype(bf16)
                ownv[b, h] = jnp.transpose(vals).astype(bf16)

    def prepare_table():
        lane = lax.broadcasted_iota(jnp.int32, (8, 128), 1)
        sub = lax.broadcasted_iota(jnp.int32, (8, 128), 0)
        table = jnp.zeros((8, 128), jnp.int32)
        for b in range(2):
            for l in range(8):
                code = jnp.where(l < depth_s[b], 4 * owner_s[b, l] + slot_s[b, l] + 1, 0)
                table = jnp.where((lane == l) & (sub == b), code, table)
        tx[3] = table
        tz[0] = table

    root_in.wait()
    prepare_root()
    pl.semaphore_wait(bar, len(peers))

    started = []

    def go(copy):
        copy.start()
        started.append(copy)

    def view(piece, pos, core):
        dz = POS_DZ[pos] % ZN
        if piece < 2:
            return qb1.at[2 * dz + piece]
        return (k0, v0, rk0, rv0)[piece - 2].at[dz, core]

    def zcopy(piece, direction, step):
        if step > 1:
            src = view(piece, pos_of(step - 1, direction), 0)
        elif piece < 2:
            src = q_hbm.at[piece, :, pl.ds(1024, 1024)]
        else:
            src = view(piece, 0, 0)
        return remote(
            src, view(piece, pos_of(step, direction), 0), zsend.at[piece, direction, step - 1],
            zrecv.at[piece, direction, step - 1], up if direction == 0 else down,
        )

    def ccopy(piece, pos):
        return remote(view(piece, pos, 0), view(piece, pos, 1), csend.at[piece, pos], crecv.at[piece, pos], other)

    def send_own(kind, which):
        for direction in (0, 1):
            go(zcopy(2 * kind + (which ^ direction), direction, 1))

    def hop(kind, which, step):
        for direction in (0, 1):
            piece = 2 * kind + (which ^ direction)
            zcopy(piece, direction, step).wait_recv()
            if step < 3 or (step == 3 and which == 0):
                go(zcopy(piece, direction, step + 1))
            if kind > 0:
                go(ccopy(piece, pos_of(step, direction)))

    def settle(kind):
        for pos in range(ZN):
            for piece in (2 * kind, 2 * kind + 1):
                ccopy(piece, pos).wait_recv()

    xrefs = (k1, v1, rk1, rv1)

    def xcopy(piece, dx):
        there = 4 - dx
        return remote(
            xrefs[piece].at[0, 0], xrefs[piece].at[there, 0], xsend.at[piece, dx - 1], xrecv.at[piece, there - 1], dev(dx=dx)
        )

    def dcopy(piece, rel):
        ref = xrefs[piece]
        return remote(ref.at[rel, 0], ref.at[rel, 1], dsend.at[piece, rel], drecv.at[piece, rel], other)

    def slot_dx(j):
        return jnp.where(j == 0, 2, 2 * j - 1)

    def slot_there(j):
        return lax.rem(3 - j, 3)

    def split(u):
        return jnp.where(u < 6, lax.rem(u, 3), 3), jnp.where(u < 6, lax.div(u, 3), u - 6)

    def qcopy(j, b):
        there = (3 - j) % 3
        return remote(
            q_hbm.at[b, :, pl.ds(0, 1024)], qb0.at[3 * b + there], qsend.at[j, b], qrecv.at[there, b], dev(dx=SLOT_DX[j])
        )

    def tcopy(j):
        there = (3 - j) % 3
        return remote(tx.at[3], tx.at[there], tsend.at[j], trecv.at[there], dev(dx=SLOT_DX[j]))

    def ucopy(dz):
        return remote(tz.at[0], tz.at[8 - dz], usend.at[dz - 1], urecv.at[7 - dz], dev(dz=dz))

    send_own(0, 0)
    send_own(0, 1)
    send_own(2, 0)
    send_own(2, 1)
    node_in.wait()
    prepare_nodes(1, k1, v1)
    for piece in (0, 1):
        for dx in (1, 3, 2):
            go(xcopy(piece, dx))
    hop(0, 0, 1)
    hop(0, 1, 1)
    prepare_nodes(0, k0, v0)
    send_own(1, 0)
    for piece in (2, 3):
        for dx in (1, 3, 2):
            go(xcopy(piece, dx))
    for copy in small_in:
        copy.wait()
    prepare_table()
    for dz in range(1, 8):
        go(ucopy(dz))
    hop(0, 0, 2)
    hop(0, 1, 2)
    for j in range(3):
        go(tcopy(j))
    for b in range(2):
        for j in (1, 2, 0):
            go(qcopy(j, b))
    for piece in range(4):
        go(dcopy(piece, 0))
        go(ccopy(2 + piece, 0))
    own_in.wait()
    prepare_own()
    hop(0, 0, 3)
    send_own(1, 1)
    hop(2, 0, 1)
    hop(2, 1, 1)
    hop(1, 0, 1)
    for copy in q_in:
        copy.wait()

    qbs, accs, mds = (qb0, qb1), (acc0, acc1), (md0, md1)

    def queries_of(u, h):
        return jnp.concatenate([qbs[h][u, :, g * 128 : g * 128 + 128] for g in range(GROUP)], axis=0)

    def scores_of(keys, q):
        return lax.dot_general(keys, q, (((1,), (1,)), ((), ())), preferred_element_type=f32)

    def with_ones(vt):
        return jnp.concatenate([vt, jnp.ones((TAIL, vt.shape[1]), bf16)], axis=0)

    def clear(h):
        def body(u, _):
            accs[h][u] = jnp.zeros((DIM + TAIL, ROWS), f32)
            mds[h][u] = jnp.full((8, ROWS), NEG, f32)
            return 0

        return body

    lax.fori_loop(0, 6, clear(0), 0)
    lax.fori_loop(2, 16, clear(1), 0)
    for piece in (0, 1, 2, 3):
        for dx in (1, 3, 2):
            xcopy(piece, dx).wait_recv()
            go(dcopy(piece, 4 - dx))
    hop(0, 1, 3)
    key_at = lax.broadcasted_iota(jnp.int32, (128, ROWS), 0)
    query_at = lax.rem(lax.broadcasted_iota(jnp.int32, (128, ROWS), 1), SEG)
    causal = key_at <= query_at
    for b in range(2):
        for h in range(2):
            u = (6 + b, b)[h]
            s = scores_of(ownk[b, h], queries_of(u, h))
            s = jnp.where(causal, s, NEG)
            m = jnp.max(s, axis=0, keepdims=True)
            p = jnp.exp2(s * C2 - m * C2).astype(bf16)
            accs[h][u] = jnp.dot(with_ones(ownv[b, h]), p, preferred_element_type=f32)
            mds[h][u] = jnp.broadcast_to(m, (8, ROWS))
    for dz in range(1, 8):
        ucopy(dz).wait_recv()
    for j in range(3):
        tcopy((3 - j) % 3).wait_recv()
    t_in = [local(10, tx, txs), local(11, tz, tzs)]
    hop(0, 0, 4)
    for copy in t_in:
        copy.wait()
    for piece in range(4):
        for rel in range(4):
            dcopy(piece, rel).wait_recv()

    def turn(vr, vt, n):
        for p in range(n):
            pair = jnp.concatenate([vr[p, 0], vr[p, 1]], axis=0).astype(f32)
            vt[p] = jnp.transpose(pair).astype(bf16)

    turn(rv1, rvt1, 4)

    sbuf, rbuf = (s0, s1), (r0, r1)

    def unit_a(u, h, t, keys, biases):
        q = queries_of(u, h)
        old = mds[h][u, 0:1, :]
        top = old
        for i in range(0, len(keys), 2):
            s = scores_of(jnp.concatenate(keys[i : i + 2], axis=0), q)
            sbuf[t][i * 128 : i * 128 + 256, :] = s
            for n in range(2):
                best = jnp.max(s[n * 128 : n * 128 + 128], axis=0, keepdims=True)
                top = jnp.maximum(top, best if biases[i + n] is None else best + biases[i + n])
        mds[h][u, 0:1, :] = top
        rbuf[t][0:1, :] = top * C2
        rbuf[t][1:2, :] = jnp.exp2((old - top) * C2)

    def unit_b(u, h, t, vts, biases):
        low, factor = rbuf[t][0:1, :], rbuf[t][1:2, :]
        weights = []
        for i, bias in enumerate(biases):
            less = low if bias is None else low - bias
            weights.append(jnp.exp2(sbuf[t][i * 128 : i * 128 + 128, :] * C2 - less).astype(bf16))
        p = jnp.concatenate(weights, axis=0)
        vt = jnp.concatenate(vts, axis=1)
        accs[h][u] = accs[h][u] * factor + jnp.dot(with_ones(vt), p, preferred_element_type=f32)

    def pipeline(count, unit_1, unit_2, after=None, hooks=()):
        unit_1(0, 0)

        def body(j, _):
            unit_1(2 * j + 1, 1)
            unit_2(2 * j, 0)
            if after is not None:
                after(2 * j)
            unit_1(2 * j + 2, 0)
            unit_2(2 * j + 1, 1)
            if after is not None:
                after(2 * j + 1)
            return 0

        at = 0
        for when, hook in hooks:
            lax.fori_loop(at, when, body, 0)
            hook()
            at = when
        lax.fori_loop(at, count // 2 - 1, body, 0)
        unit_1(count - 1, 1)
        unit_2(count - 2, 0)
        unit_2(count - 1, 1)

    def bias_of(active):
        return jnp.where(active, 0.0, NEG).astype(f32)

    def pairs(ref, n):
        return [jnp.concatenate([ref[p, 0], ref[p, 1]], axis=0) for p in range(n)]

    def slot_of(code):
        return jnp.clip((code & 3) - 1, 0, SLOTS - 1)

    def column_stage(after, hooks=()):
        def names(u):
            j, b = split(u)
            got, biases = [], [None] * ZN
            for l in range(8):
                code = txs[j, b, l]
                owner = code >> 2
                biases.append(bias_of((code > 0) & (((owner >> 1) & (XN - 1)) == x)))
                got.append((((owner >> 3) - z + ZN) & (ZN - 1), (owner + c) & 1, slot_of(code)))
            return got, biases

        def first(u, t):
            at, biases = names(u)
            unit_a(u, 0, t, pairs(rk0, ZN) + [k0[a] for a in at], biases)

        def second(u, t):
            at, biases = names(u)
            unit_b(u, 0, t, [rvt0[p] for p in range(ZN)] + [v0[a] for a in at], biases)

        pipeline(8, first, second, after, hooks)

    def row_stage(hooks=()):
        def names(u):
            got, biases = [], [None] * XN
            for l in range(8):
                code = tzs[u // 2, u % 2, l]
                owner = code >> 2
                biases.append(bias_of((code > 0) & ((owner >> 3) == z)))
                got.append((((owner >> 1) - x + XN) & (XN - 1), (owner + c) & 1, slot_of(code)))
            return got, biases

        def first(u, t):
            at, biases = names(u)
            unit_a(u, 1, t, pairs(rk1, XN) + [k1[a] for a in at], biases)

        def second(u, t):
            at, biases = names(u)
            unit_b(u, 1, t, [rvt1[p] for p in range(XN)] + [v1[a] for a in at], biases)

        pipeline(16, first, second, None, hooks)

    def three(v):
        a = v.astype(bf16).astype(f32)
        b = (v - a).astype(bf16).astype(f32)
        return [a, b, v - a - b]

    def write(ref, total, top, den):
        ref[:DIM, :] = total.astype(bf16)
        tail = jnp.concatenate(three(top) + three(den) + [jnp.zeros((TAIL - 6, ROWS), f32)], axis=0)
        ref[DIM:, :] = tail.astype(bf16)

    def read(ref):
        tail = ref[DIM:, :].astype(f32)
        return ref[:DIM, :].astype(f32), tail[0:1] + tail[1:2] + tail[2:3], tail[3:4] + tail[4:5] + tail[5:6]

    def state(h, u):
        return accs[h][u, :DIM, :], mds[h][u, 0:1, :], accs[h][u, DIM : DIM + 1, :]

    def combine(parts):
        top = functools.reduce(jnp.maximum, [p[1] for p in parts])
        ws = [jnp.exp2((p[1] - top) * C2) for p in parts]
        return ws, top, sum(w * p[2] for w, p in zip(ws, parts))

    def ocopy(j, b):
        there = slot_there(j)
        return remote(send0.at[j, b], recv0.at[there, b], osend.at[j, b], orecv.at[there, b], dev(dx=slot_dx(j)))

    def send_part(u):
        j, b = split(u)
        write(send0.at[j, b], *state(0, u))
        ocopy(j, b).start()

    def pcopy(direction, step, b):
        return remote(
            send1.at[direction, step - 1, b], recv1.at[direction, step - 1, b], psend.at[direction, step - 1, b],
            precv.at[direction, step - 1, b], up if direction == 0 else down,
        )

    def pass_on(step, fresh):
        for direction in (0, 1):
            b = direction ^ fresh
            away = 5 - step if direction == 0 else 3 + step
            mine = state(1, 2 * away + b)
            if step > 2 or (step == 2 and fresh == 0):
                pcopy(direction, step - 1, b).wait_recv()
                parts = [mine, read(recv1.at[direction, step - 2, b])]
                ws, top, den = combine(parts)
                mine = (sum(w * p[0] for w, p in zip(ws, parts)), top, den)
            write(send1.at[direction, step - 1, b], *mine)
            go(pcopy(direction, step, b))

    def finish(h, b, u, parts):
        ws, top, den = combine(parts)
        inv = 1.0 / den
        total = sum(p[0] * (w * inv) for w, p in zip(ws, parts))
        live = lax.rem(lax.broadcasted_iota(jnp.int32, (1, ROWS), 1), SEG) < seg_s[b]
        total = jnp.where(live, total, 0.0)
        part = jnp.sum(total * total, axis=0, keepdims=True)
        ssq[b : b + 1, :] = part if h == 0 else ssq[b : b + 1, :] + part
        accs[h][u, :DIM, :] = total

    def place(h, b, u):
        rows = jnp.transpose(accs[h][u, :DIM, :])
        for g in range(GROUP):
            at = h * 1024 + g * 128
            gain = gain_ref[at : at + 128].astype(f32).reshape(1, DIM)
            att[b, :, at : at + 128] = rows[g * SEG : g * SEG + SEG, :] * gain

    def merge0(b):
        for j in range(3):
            ocopy((3 - j) % 3, b).wait_recv()
        finish(0, b, 6 + b, [state(0, 6 + b)] + [read(recv0.at[j, b]) for j in range(3)])

    def merge1(b):
        for direction in (0, 1):
            pcopy(direction, 4, b).wait_recv()
        finish(1, b, b, [state(1, b)] + [read(recv1.at[direction, 3, b]) for direction in (0, 1)])

    def hook_root():
        hop(2, 0, 2)
        hop(2, 1, 2)

    row_stage([(2, lambda: hop(1, 1, 1)), (3, hook_root), (5, lambda: hop(1, 0, 2))])
    hop(1, 1, 2)
    hop(2, 0, 3)
    hop(2, 1, 3)
    hop(1, 0, 3)
    pass_on(1, 0)
    pass_on(2, 1)
    hop(1, 1, 3)
    for j in range(3):
        for b in range(2):
            qcopy((3 - j) % 3, b).wait_recv()
    hop(2, 0, 4)
    settle(2)
    turn(rv0, rvt0, ZN)
    hop(1, 0, 4)
    pass_on(2, 0)
    settle(1)
    column_stage(send_part, [(1, lambda: pass_on(3, 1)), (2, lambda: pass_on(3, 0)), (3, lambda: pass_on(4, 1))])
    pass_on(4, 0)
    gain_in.wait()
    for b in range(2):
        merge0(b)
    for b in range(2):
        place(0, b, 6 + b)
    merge1(0)
    merge1(1)

    def ycopy(d):
        return pltpu.make_async_remote_copy(
            ssq, ssq_in.at[3 - d], ysend.at[d - 1], yrecv.at[3 - d], device_id=dev(dy=d), device_id_type=MESH
        )

    for d in (1, 2, 3):
        go(ycopy(d))
    for b in range(2):
        place(1, b, b)
    for d in (1, 2, 3):
        ycopy(d).wait_recv()
    squares = jnp.transpose(ssq[...] + ssq_in[0] + ssq_in[1] + ssq_in[2])
    squares = sum(squares[g * SEG : g * SEG + SEG, :] for g in range(GROUP))
    scales = lax.rsqrt(squares / (HEADS * DIM) + 1e-6)
    for b in range(2):
        scale = scales[:, b : b + 1]
        for g in range(2 * GROUP):
            at = slice(g * 128, g * 128 + 128)
            out_ref[b, :, at] = (att[b, :, at] * scale).astype(bf16)

    for copy in started:
        copy.wait_send()
    for j in range(3):
        for b in range(2):
            ocopy(j, b).wait_send()


def on_device(queries, root_kv, node_kv, own_kv, anc_owner, anc_slot, depth_len, seg_len, norm_gain):
    bf16, f32 = jnp.bfloat16, jnp.float32

    def rows_of(kv):
        lead = kv.shape[:-2]
        n = len(lead)
        kv = kv.reshape(lead + (2, 2, DIM))
        kv = kv.transpose(tuple(range(n)) + (n + 1, n, n + 2))
        return kv.reshape(-1, DIM)

    dma = pltpu.SemaphoreType.DMA
    scratch = [
        pltpu.VMEM((2 * 2 * ROOT, DIM), bf16),
        pltpu.VMEM((SLOTS * 2 * 2 * 128, DIM), bf16),
        pltpu.VMEM((2 * 2 * 2 * SEG, DIM), bf16),
        pltpu.SMEM((2, 8), jnp.int32),
        pltpu.SMEM((2, 8), jnp.int32),
        pltpu.SMEM((2,), jnp.int32),
        pltpu.SMEM((2,), jnp.int32),
        pltpu.VMEM((2048,), bf16),
        pltpu.VMEM((8, SEG, 1024), bf16),
        pltpu.VMEM((16, SEG, 1024), bf16),
        pltpu.VMEM((ZN, 2, ROOT, DIM), bf16),
        pltpu.VMEM((ZN, 2, ROOT, DIM), bf16),
        pltpu.VMEM((ZN, DIM, 2 * ROOT), bf16),
        pltpu.VMEM((XN, 2, ROOT, DIM), bf16),
        pltpu.VMEM((XN, 2, ROOT, DIM), bf16),
        pltpu.VMEM((XN, DIM, 2 * ROOT), bf16),
        pltpu.VMEM((2, 2, 128, DIM), bf16),
        pltpu.VMEM((2, 2, DIM, 128), bf16),
        pltpu.VMEM((ZN, 2, SLOTS, 128, DIM), bf16),
        pltpu.VMEM((ZN, 2, SLOTS, DIM, 128), bf16),
        pltpu.VMEM((XN, 2, SLOTS, 128, DIM), bf16),
        pltpu.VMEM((XN, 2, SLOTS, DIM, 128), bf16),
        pltpu.VMEM((8, DIM + TAIL, ROWS), f32),
        pltpu.VMEM((16, DIM + TAIL, ROWS), f32),
        pltpu.VMEM((8, 8, ROWS), f32),
        pltpu.VMEM((16, 8, ROWS), f32),
        pltpu.VMEM((2048, ROWS), f32),
        pltpu.VMEM((2048, ROWS), f32),
        pltpu.VMEM((8, ROWS), f32),
        pltpu.VMEM((8, ROWS), f32),
        pltpu.VMEM((XN, 8, 128), jnp.int32),
        pltpu.VMEM((ZN, 8, 128), jnp.int32),
        pltpu.SMEM((XN, 8, 128), jnp.int32),
        pltpu.SMEM((ZN, 8, 128), jnp.int32),
        pltpu.VMEM((3, 2, DIM + TAIL, ROWS), bf16),
        pltpu.VMEM((3, 2, DIM + TAIL, ROWS), bf16),
        pltpu.VMEM((2, 4, 2, DIM + TAIL, ROWS), bf16),
        pltpu.VMEM((2, 4, 2, DIM + TAIL, ROWS), bf16),
        pltpu.VMEM((2, SEG, 2048), f32),
        pltpu.VMEM((8, ROWS), f32),
        pltpu.VMEM((3, 8, ROWS), f32),
    ]
    for shape in ((NRING, 2, 4), (NRING, 8), (4, 3), (4, 4), (3, 2), (3,), (7,), (3, 2), (2, 4, 2), (3,)):
        scratch += [dma(shape), dma(shape)]
    scratch.append(dma((12,)))
    return pl.pallas_call(
        kernel,
        out_shape=jax.ShapeDtypeStruct(queries.shape, bf16),
        in_specs=[pl.BlockSpec(memory_space=pltpu.HBM)] * 9,
        out_specs=pl.BlockSpec(memory_space=pltpu.VMEM),
        scratch_shapes=scratch,
        compiler_params=pltpu.CompilerParams(
            collective_id=0, has_side_effects=True, vmem_limit_bytes=48 * 2**20
        ),
        name="tree_attention",
    )(
        *[
            pltpu.with_memory_space_constraint(v, pltpu.HBM)
            for v in (
                queries, rows_of(root_kv), rows_of(node_kv), rows_of(own_kv),
                anc_owner, anc_slot, depth_len, seg_len, norm_gain,
            )
        ]
    )


def solution(mesh):
    in_specs = (
        P("branch", None, "blk"),
        P("branch", None, "blk"),
        P("branch", None, None, "blk"),
        P("branch", None, None, "blk"),
        P("branch", None),
        P("branch", None),
        P("branch"),
        P("branch"),
        P("blk"),
    )
    return jax.shard_map(
        on_device, mesh=mesh, in_specs=in_specs, out_specs=P("branch", None, "blk"), check_vma=False
    )
```

```python
import functools
import math

import jax
import jax.numpy as jnp
from jax import lax
from jax.experimental import pallas as pl
from jax.experimental.pallas import tpu as pltpu
from jax.sharding import PartitionSpec as P

MESH = pl.DeviceIdType.MESH
HEADS = 64
DIM = 128
SEG = 32
GROUP = 8
SLOTS = 3
ROWS = GROUP * SEG
ROOT = 64
ZN = 8
XN = 4
C2 = math.log2(math.e) / math.sqrt(DIM)
NEG = -1e30
TAIL = 16
POS_DZ = (0, -1, 1, -2, 2, -3, 3, 4)
SLOT_DX = (2, 1, 3)
NRING = 6


def pos_of(step, direction):
    return 7 if step == 4 else 2 * step - 1 + direction


def kernel(
    q_hbm, root_hbm, node_hbm, own_hbm, owner_hbm, slot_hbm, depth_hbm, seg_hbm, gain_hbm, out_ref,
    root_x, node_x, own_x, owner_s, slot_s, depth_s, seg_s, gain_ref,
    qb0, qb1, rk0, rv0, rvt0, rk1, rv1, rvt1, ownk, ownv, k0, v0, k1, v1,
    acc0, acc1, md0, md1, s0, s1, r0, r1, tx, tz, txs, tzs, send0, recv0, send1, recv1, att, ssq, ssq_in,
    zsend, zrecv, csend, crecv, xsend, xrecv, dsend, drecv, qsend, qrecv, tsend, trecv, usend, urecv,
    osend, orecv, psend, precv, ysend, yrecv, lsem,
):
    bf16, f32 = jnp.bfloat16, jnp.float32
    y = lax.axis_index("blk")
    r = lax.axis_index("branch")
    z, x, c = r // 8, (r // 2) % 4, r % 2

    def dev(dy=0, dz=0, dx=0, dc=0):
        zz = lax.rem(z + dz + ZN, ZN)
        xx = lax.rem(x + dx + XN, XN)
        cc = lax.rem(c + dc, 2)
        return (lax.rem(y + dy, 4), zz * 8 + xx * 2 + cc)

    def remote(src, dst, ssem, rsem, to):
        return pltpu.make_async_remote_copy(src, dst, ssem, rsem, device_id=to, device_id_type=MESH)

    bar = pltpu.get_barrier_semaphore()
    up, down, other = dev(dz=1), dev(dz=-1), dev(dc=1)
    peers = [other] + [dev(dz=d) for d in range(1, 8)]
    peers += [dev(dx=d) for d in (1, 2, 3)] + [dev(dy=d) for d in (1, 2, 3)]
    for p in peers:
        pl.semaphore_signal(bar, inc=1, device_id=p, device_id_type=MESH)

    def local(i, src, dst):
        copy = pltpu.make_async_copy(src, dst, lsem.at[i])
        copy.start()
        return copy

    root_in = local(1, root_hbm, root_x)
    node_in = local(0, node_hbm, node_x)
    small_in = [
        local(2, owner_hbm, owner_s), local(3, slot_hbm, slot_s), local(4, depth_hbm, depth_s), local(5, seg_hbm, seg_s)
    ]
    q_in = [
        local(6, q_hbm.at[:, :, pl.ds(0, 1024)], qb0.at[pl.ds(6, 2)]),
        local(9, q_hbm.at[:, :, pl.ds(1024, 1024)], qb1.at[pl.ds(0, 2)]),
    ]
    own_in = local(7, own_hbm, own_x)
    gain_in = local(8, gain_hbm, gain_ref)

    row = lax.broadcasted_iota(jnp.int32, (128, 128), 0)
    col = lax.broadcasted_iota(jnp.int32, (128, 128), 1)
    want = (row % 32) * 4 + row // 32
    pick = jnp.where(col == want, 1.0, 0.0).astype(bf16)

    def apart(ref, first):
        return jnp.dot(pick, ref[first : first + 128, :], preferred_element_type=f32)

    def prepare_root():
        got = [apart(root_x, t * 128).astype(bf16) for t in range(2)]
        for h, (kr, vr) in enumerate(((rk0, rv0), (rk1, rv1))):
            for t in range(2):
                kr[0, 0, t * 32 : t * 32 + 32, :] = got[t][h * 64 : h * 64 + 32]
                vr[0, 0, t * 32 : t * 32 + 32, :] = got[t][h * 64 + 32 : h * 64 + 64]

    def prepare_nodes(h, kr, vr):
        for s in range(SLOTS):
            got = [apart(node_x, (s * 4 + t) * 128) for t in range(4)]
            keys = jnp.concatenate([g[h * 64 : h * 64 + 32] for g in got], axis=0)
            vals = jnp.concatenate([g[h * 64 + 32 : h * 64 + 64] for g in got], axis=0)
            kr[0, 0, s] = keys.astype(bf16)
            vr[0, 0, s] = jnp.transpose(vals).astype(bf16)

    def prepare_own():
        zeros96 = jnp.zeros((96, 128), f32)
        for b in range(2):
            got = apart(own_x, b * 128)
            for h in range(2):
                keys = jnp.concatenate([got[h * 64 : h * 64 + 32], zeros96], axis=0)
                vals = jnp.concatenate([got[h * 64 + 32 : h * 64 + 64], zeros96], axis=0)
                ownk[b, h] = keys.astype(bf16)
                ownv[b, h] = jnp.transpose(vals).astype(bf16)

    def prepare_table():
        lane = lax.broadcasted_iota(jnp.int32, (8, 128), 1)
        sub = lax.broadcasted_iota(jnp.int32, (8, 128), 0)
        table = jnp.zeros((8, 128), jnp.int32)
        for b in range(2):
            for l in range(8):
                code = jnp.where(l < depth_s[b], 4 * owner_s[b, l] + slot_s[b, l] + 1, 0)
                table = jnp.where((lane == l) & (sub == b), code, table)
        tx[3] = table
        tz[0] = table

    root_in.wait()
    prepare_root()
    pl.semaphore_wait(bar, len(peers))

    started = []

    def go(copy):
        copy.start()
        started.append(copy)

    def view(piece, pos, core):
        dz = POS_DZ[pos] % ZN
        if piece < 2:
            return qb1.at[2 * dz + piece]
        return (k0, v0, rk0, rv0)[piece - 2].at[dz, core]

    def zcopy(piece, direction, step):
        if step > 1:
            src = view(piece, pos_of(step - 1, direction), 0)
        elif piece < 2:
            src = q_hbm.at[piece, :, pl.ds(1024, 1024)]
        else:
            src = view(piece, 0, 0)
        return remote(
            src, view(piece, pos_of(step, direction), 0), zsend.at[piece, direction, step - 1],
            zrecv.at[piece, direction, step - 1], up if direction == 0 else down,
        )

    def ccopy(piece, pos):
        return remote(view(piece, pos, 0), view(piece, pos, 1), csend.at[piece, pos], crecv.at[piece, pos], other)

    def send_own(kind, which):
        for direction in (0, 1):
            go(zcopy(2 * kind + (which ^ direction), direction, 1))

    def hop(kind, which, step):
        for direction in (0, 1):
            piece = 2 * kind + (which ^ direction)
            zcopy(piece, direction, step).wait_recv()
            if step < 3 or (step == 3 and which == 0):
                go(zcopy(piece, direction, step + 1))
            if kind > 0:
                go(ccopy(piece, pos_of(step, direction)))

    def settle(kind):
        for pos in range(ZN):
            for piece in (2 * kind, 2 * kind + 1):
                ccopy(piece, pos).wait_recv()

    xrefs = (k1, v1, rk1, rv1)

    def xcopy(piece, dx):
        there = 4 - dx
        return remote(
            xrefs[piece].at[0, 0], xrefs[piece].at[there, 0], xsend.at[piece, dx - 1], xrecv.at[piece, there - 1], dev(dx=dx)
        )

    def dcopy(piece, rel):
        ref = xrefs[piece]
        return remote(ref.at[rel, 0], ref.at[rel, 1], dsend.at[piece, rel], drecv.at[piece, rel], other)

    def slot_dx(j):
        return jnp.where(j == 0, 2, 2 * j - 1)

    def slot_there(j):
        return lax.rem(3 - j, 3)

    def split(u):
        return jnp.where(u < 6, lax.rem(u, 3), 3), jnp.where(u < 6, lax.div(u, 3), u - 6)

    def qcopy(j, b):
        there = (3 - j) % 3
        return remote(
            q_hbm.at[b, :, pl.ds(0, 1024)], qb0.at[3 * b + there], qsend.at[j, b], qrecv.at[there, b], dev(dx=SLOT_DX[j])
        )

    def tcopy(j):
        there = (3 - j) % 3
        return remote(tx.at[3], tx.at[there], tsend.at[j], trecv.at[there], dev(dx=SLOT_DX[j]))

    def ucopy(dz):
        return remote(tz.at[0], tz.at[8 - dz], usend.at[dz - 1], urecv.at[7 - dz], dev(dz=dz))

    send_own(0, 0)
    send_own(0, 1)
    send_own(2, 0)
    send_own(2, 1)
    node_in.wait()
    prepare_nodes(1, k1, v1)
    for piece in (0, 1):
        for dx in (1, 3, 2):
            go(xcopy(piece, dx))
    hop(0, 0, 1)
    hop(0, 1, 1)
    prepare_nodes(0, k0, v0)
    send_own(1, 0)
    for piece in (2, 3):
        for dx in (1, 3, 2):
            go(xcopy(piece, dx))
    for copy in small_in:
        copy.wait()
    prepare_table()
    for dz in range(1, 8):
        go(ucopy(dz))
    hop(0, 0, 2)
    hop(0, 1, 2)
    for j in range(3):
        go(tcopy(j))
    for b in range(2):
        for j in (1, 2, 0):
            go(qcopy(j, b))
    for piece in range(4):
        go(dcopy(piece, 0))
        go(ccopy(2 + piece, 0))
    own_in.wait()
    prepare_own()
    hop(0, 0, 3)
    send_own(1, 1)
    hop(2, 0, 1)
    hop(2, 1, 1)
    hop(1, 0, 1)
    for copy in q_in:
        copy.wait()

    qbs, accs, mds = (qb0, qb1), (acc0, acc1), (md0, md1)

    def queries_of(u, h):
        return jnp.concatenate([qbs[h][u, :, g * 128 : g * 128 + 128] for g in range(GROUP)], axis=0)

    def scores_of(keys, q):
        return lax.dot_general(keys, q, (((1,), (1,)), ((), ())), preferred_element_type=f32)

    def with_ones(vt):
        return jnp.concatenate([vt, jnp.ones((TAIL, vt.shape[1]), bf16)], axis=0)

    def clear(h):
        def body(u, _):
            accs[h][u] = jnp.zeros((DIM + TAIL, ROWS), f32)
            mds[h][u] = jnp.full((8, ROWS), NEG, f32)
            return 0

        return body

    lax.fori_loop(0, 6, clear(0), 0)
    lax.fori_loop(2, 16, clear(1), 0)
    for piece in (0, 1, 2, 3):
        for dx in (1, 3, 2):
            xcopy(piece, dx).wait_recv()
            go(dcopy(piece, 4 - dx))
    hop(0, 1, 3)
    key_at = lax.broadcasted_iota(jnp.int32, (128, ROWS), 0)
    query_at = lax.rem(lax.broadcasted_iota(jnp.int32, (128, ROWS), 1), SEG)
    causal = key_at <= query_at
    for b in range(2):
        for h in range(2):
            u = (6 + b, b)[h]
            s = scores_of(ownk[b, h], queries_of(u, h))
            s = jnp.where(causal, s, NEG)
            m = jnp.max(s, axis=0, keepdims=True)
            p = jnp.exp2(s * C2 - m * C2).astype(bf16)
            accs[h][u] = jnp.dot(with_ones(ownv[b, h]), p, preferred_element_type=f32)
            mds[h][u] = jnp.broadcast_to(m, (8, ROWS))
    for dz in range(1, 8):
        ucopy(dz).wait_recv()
    for j in range(3):
        tcopy((3 - j) % 3).wait_recv()
    t_in = [local(10, tx, txs), local(11, tz, tzs)]
    hop(0, 0, 4)
    for copy in t_in:
        copy.wait()
    for piece in range(4):
        for rel in range(4):
            dcopy(piece, rel).wait_recv()

    def turn(vr, vt, n):
        for p in range(n):
            pair = jnp.concatenate([vr[p, 0], vr[p, 1]], axis=0).astype(f32)
            vt[p] = jnp.transpose(pair).astype(bf16)

    turn(rv1, rvt1, 4)

    sbuf, rbuf = (s0, s1), (r0, r1)

    def unit_a(u, h, t, keys, biases):
        q = queries_of(u, h)
        old = mds[h][u, 0:1, :]
        top = old
        for i in range(0, len(keys), 2):
            s = scores_of(jnp.concatenate(keys[i : i + 2], axis=0), q)
            sbuf[t][i * 128 : i * 128 + 256, :] = s
            for n in range(2):
                best = jnp.max(s[n * 128 : n * 128 + 128], axis=0, keepdims=True)
                top = jnp.maximum(top, best if biases[i + n] is None else best + biases[i + n])
        mds[h][u, 0:1, :] = top
        rbuf[t][0:1, :] = top * C2
        rbuf[t][1:2, :] = jnp.exp2((old - top) * C2)

    def unit_b(u, h, t, vts, biases):
        low, factor = rbuf[t][0:1, :], rbuf[t][1:2, :]
        weights = []
        for i, bias in enumerate(biases):
            less = low if bias is None else low - bias
            weights.append(jnp.exp2(sbuf[t][i * 128 : i * 128 + 128, :] * C2 - less).astype(bf16))
        p = jnp.concatenate(weights, axis=0)
        vt = jnp.concatenate(vts, axis=1)
        accs[h][u] = accs[h][u] * factor + jnp.dot(with_ones(vt), p, preferred_element_type=f32)

    def pipeline(count, unit_1, unit_2, after=None, hooks=()):
        unit_1(0, 0)

        def body(j, _):
            unit_1(2 * j + 1, 1)
            unit_2(2 * j, 0)
            if after is not None:
                after(2 * j)
            unit_1(2 * j + 2, 0)
            unit_2(2 * j + 1, 1)
            if after is not None:
                after(2 * j + 1)
            return 0

        at = 0
        for when, hook in hooks:
            lax.fori_loop(at, when, body, 0)
            hook()
            at = when
        lax.fori_loop(at, count // 2 - 1, body, 0)
        unit_1(count - 1, 1)
        unit_2(count - 2, 0)
        unit_2(count - 1, 1)

    def bias_of(active):
        return jnp.where(active, 0.0, NEG).astype(f32)

    def pairs(ref, n):
        return [jnp.concatenate([ref[p, 0], ref[p, 1]], axis=0) for p in range(n)]

    def slot_of(code):
        return jnp.clip((code & 3) - 1, 0, SLOTS - 1)

    def column_stage(after, hooks=()):
        def names(u):
            j, b = split(u)
            got, biases = [], [None] * ZN
            for l in range(8):
                code = txs[j, b, l]
                owner = code >> 2
                biases.append(bias_of((code > 0) & (((owner >> 1) & (XN - 1)) == x)))
                got.append((((owner >> 3) - z + ZN) & (ZN - 1), (owner + c) & 1, slot_of(code)))
            return got, biases

        def first(u, t):
            at, biases = names(u)
            unit_a(u, 0, t, pairs(rk0, ZN) + [k0[a] for a in at], biases)

        def second(u, t):
            at, biases = names(u)
            unit_b(u, 0, t, [rvt0[p] for p in range(ZN)] + [v0[a] for a in at], biases)

        pipeline(8, first, second, after, hooks)

    def row_stage(hooks=()):
        def names(u):
            got, biases = [], [None] * XN
            for l in range(8):
                code = tzs[u // 2, u % 2, l]
                owner = code >> 2
                biases.append(bias_of((code > 0) & ((owner >> 3) == z)))
                got.append((((owner >> 1) - x + XN) & (XN - 1), (owner + c) & 1, slot_of(code)))
            return got, biases

        def first(u, t):
            at, biases = names(u)
            unit_a(u, 1, t, pairs(rk1, XN) + [k1[a] for a in at], biases)

        def second(u, t):
            at, biases = names(u)
            unit_b(u, 1, t, [rvt1[p] for p in range(XN)] + [v1[a] for a in at], biases)

        pipeline(16, first, second, None, hooks)

    def three(v):
        a = v.astype(bf16).astype(f32)
        b = (v - a).astype(bf16).astype(f32)
        return [a, b, v - a - b]

    def write(ref, total, top, den):
        ref[:DIM, :] = total.astype(bf16)
        tail = jnp.concatenate(three(top) + three(den) + [jnp.zeros((TAIL - 6, ROWS), f32)], axis=0)
        ref[DIM:, :] = tail.astype(bf16)

    def read(ref):
        tail = ref[DIM:, :].astype(f32)
        return ref[:DIM, :].astype(f32), tail[0:1] + tail[1:2] + tail[2:3], tail[3:4] + tail[4:5] + tail[5:6]

    def state(h, u):
        return accs[h][u, :DIM, :], mds[h][u, 0:1, :], accs[h][u, DIM : DIM + 1, :]

    def combine(parts):
        top = functools.reduce(jnp.maximum, [p[1] for p in parts])
        ws = [jnp.exp2((p[1] - top) * C2) for p in parts]
        return ws, top, sum(w * p[2] for w, p in zip(ws, parts))

    def ocopy(j, b):
        there = slot_there(j)
        return remote(send0.at[j, b], recv0.at[there, b], osend.at[j, b], orecv.at[there, b], dev(dx=slot_dx(j)))

    def send_part(u):
        j, b = split(u)
        write(send0.at[j, b], *state(0, u))
        ocopy(j, b).start()

    def pcopy(direction, step, b):
        return remote(
            send1.at[direction, step - 1, b], recv1.at[direction, step - 1, b], psend.at[direction, step - 1, b],
            precv.at[direction, step - 1, b], up if direction == 0 else down,
        )

    def pass_on(step, fresh):
        for direction in (0, 1):
            b = direction ^ fresh
            away = 5 - step if direction == 0 else 3 + step
            mine = state(1, 2 * away + b)
            if step > 2 or (step == 2 and fresh == 0):
                pcopy(direction, step - 1, b).wait_recv()
                parts = [mine, read(recv1.at[direction, step - 2, b])]
                ws, top, den = combine(parts)
                mine = (sum(w * p[0] for w, p in zip(ws, parts)), top, den)
            write(send1.at[direction, step - 1, b], *mine)
            go(pcopy(direction, step, b))

    def finish(h, b, u, parts):
        ws, top, den = combine(parts)
        inv = 1.0 / den
        total = sum(p[0] * (w * inv) for w, p in zip(ws, parts))
        live = lax.rem(lax.broadcasted_iota(jnp.int32, (1, ROWS), 1), SEG) < seg_s[b]
        total = jnp.where(live, total, 0.0)
        part = jnp.sum(total * total, axis=0, keepdims=True)
        ssq[b : b + 1, :] = part if h == 0 else ssq[b : b + 1, :] + part
        accs[h][u, :DIM, :] = total

    def place(h, b, u):
        rows = jnp.transpose(accs[h][u, :DIM, :])
        for g in range(GROUP):
            at = h * 1024 + g * 128
            gain = gain_ref[at : at + 128].astype(f32).reshape(1, DIM)
            att[b, :, at : at + 128] = rows[g * SEG : g * SEG + SEG, :] * gain

    def merge0(b):
        for j in range(3):
            ocopy((3 - j) % 3, b).wait_recv()
        finish(0, b, 6 + b, [state(0, 6 + b)] + [read(recv0.at[j, b]) for j in range(3)])

    def merge1(b):
        for direction in (0, 1):
            pcopy(direction, 4, b).wait_recv()
        finish(1, b, b, [state(1, b)] + [read(recv1.at[direction, 3, b]) for direction in (0, 1)])

    def hook_root():
        hop(2, 0, 2)
        hop(2, 1, 2)

    row_stage([(2, lambda: hop(1, 1, 1)), (3, hook_root), (5, lambda: hop(1, 0, 2))])
    hop(1, 1, 2)
    hop(2, 0, 3)
    hop(2, 1, 3)
    hop(1, 0, 3)
    pass_on(1, 0)
    pass_on(2, 1)
    hop(1, 1, 3)
    for j in range(3):
        for b in range(2):
            qcopy((3 - j) % 3, b).wait_recv()
    hop(2, 0, 4)
    settle(2)
    turn(rv0, rvt0, ZN)
    hop(1, 0, 4)
    pass_on(2, 0)
    settle(1)
    column_stage(send_part, [(1, lambda: pass_on(3, 1)), (2, lambda: pass_on(3, 0)), (3, lambda: pass_on(4, 1))])
    pass_on(4, 0)
    gain_in.wait()
    for b in range(2):
        merge0(b)
    merge1(0)
    merge1(1)

    def ycopy(d):
        return pltpu.make_async_remote_copy(
            ssq, ssq_in.at[3 - d], ysend.at[d - 1], yrecv.at[3 - d], device_id=dev(dy=d), device_id_type=MESH
        )

    for d in (1, 2, 3):
        go(ycopy(d))
    for b in range(2):
        place(0, b, 6 + b)
        place(1, b, b)
    for d in (1, 2, 3):
        ycopy(d).wait_recv()
    squares = jnp.transpose(ssq[...] + ssq_in[0] + ssq_in[1] + ssq_in[2])
    squares = sum(squares[g * SEG : g * SEG + SEG, :] for g in range(GROUP))
    scales = lax.rsqrt(squares / (HEADS * DIM) + 1e-6)
    for b in range(2):
        scale = scales[:, b : b + 1]
        for g in range(2 * GROUP):
            at = slice(g * 128, g * 128 + 128)
            out_ref[b, :, at] = (att[b, :, at] * scale).astype(bf16)

    for copy in started:
        copy.wait_send()
    for j in range(3):
        for b in range(2):
            ocopy(j, b).wait_send()


def on_device(queries, root_kv, node_kv, own_kv, anc_owner, anc_slot, depth_len, seg_len, norm_gain):
    bf16, f32 = jnp.bfloat16, jnp.float32

    def rows_of(kv):
        lead = kv.shape[:-2]
        n = len(lead)
        kv = kv.reshape(lead + (2, 2, DIM))
        kv = kv.transpose(tuple(range(n)) + (n + 1, n, n + 2))
        return kv.reshape(-1, DIM)

    dma = pltpu.SemaphoreType.DMA
    scratch = [
        pltpu.VMEM((2 * 2 * ROOT, DIM), bf16),
        pltpu.VMEM((SLOTS * 2 * 2 * 128, DIM), bf16),
        pltpu.VMEM((2 * 2 * 2 * SEG, DIM), bf16),
        pltpu.SMEM((2, 8), jnp.int32),
        pltpu.SMEM((2, 8), jnp.int32),
        pltpu.SMEM((2,), jnp.int32),
        pltpu.SMEM((2,), jnp.int32),
        pltpu.VMEM((2048,), bf16),
        pltpu.VMEM((8, SEG, 1024), bf16),
        pltpu.VMEM((16, SEG, 1024), bf16),
        pltpu.VMEM((ZN, 2, ROOT, DIM), bf16),
        pltpu.VMEM((ZN, 2, ROOT, DIM), bf16),
        pltpu.VMEM((ZN, DIM, 2 * ROOT), bf16),
        pltpu.VMEM((XN, 2, ROOT, DIM), bf16),
        pltpu.VMEM((XN, 2, ROOT, DIM), bf16),
        pltpu.VMEM((XN, DIM, 2 * ROOT), bf16),
        pltpu.VMEM((2, 2, 128, DIM), bf16),
        pltpu.VMEM((2, 2, DIM, 128), bf16),
        pltpu.VMEM((ZN, 2, SLOTS, 128, DIM), bf16),
        pltpu.VMEM((ZN, 2, SLOTS, DIM, 128), bf16),
        pltpu.VMEM((XN, 2, SLOTS, 128, DIM), bf16),
        pltpu.VMEM((XN, 2, SLOTS, DIM, 128), bf16),
        pltpu.VMEM((8, DIM + TAIL, ROWS), f32),
        pltpu.VMEM((16, DIM + TAIL, ROWS), f32),
        pltpu.VMEM((8, 8, ROWS), f32),
        pltpu.VMEM((16, 8, ROWS), f32),
        pltpu.VMEM((2048, ROWS), f32),
        pltpu.VMEM((2048, ROWS), f32),
        pltpu.VMEM((8, ROWS), f32),
        pltpu.VMEM((8, ROWS), f32),
        pltpu.VMEM((XN, 8, 128), jnp.int32),
        pltpu.VMEM((ZN, 8, 128), jnp.int32),
        pltpu.SMEM((XN, 8, 128), jnp.int32),
        pltpu.SMEM((ZN, 8, 128), jnp.int32),
        pltpu.VMEM((3, 2, DIM + TAIL, ROWS), bf16),
        pltpu.VMEM((3, 2, DIM + TAIL, ROWS), bf16),
        pltpu.VMEM((2, 4, 2, DIM + TAIL, ROWS), bf16),
        pltpu.VMEM((2, 4, 2, DIM + TAIL, ROWS), bf16),
        pltpu.VMEM((2, SEG, 2048), f32),
        pltpu.VMEM((8, ROWS), f32),
        pltpu.VMEM((3, 8, ROWS), f32),
    ]
    for shape in ((NRING, 2, 4), (NRING, 8), (4, 3), (4, 4), (3, 2), (3,), (7,), (3, 2), (2, 4, 2), (3,)):
        scratch += [dma(shape), dma(shape)]
    scratch.append(dma((12,)))
    return pl.pallas_call(
        kernel,
        out_shape=jax.ShapeDtypeStruct(queries.shape, bf16),
        in_specs=[pl.BlockSpec(memory_space=pltpu.HBM)] * 9,
        out_specs=pl.BlockSpec(memory_space=pltpu.VMEM),
        scratch_shapes=scratch,
        compiler_params=pltpu.CompilerParams(
            collective_id=0, has_side_effects=True, vmem_limit_bytes=48 * 2**20
        ),
        name="tree_attention",
    )(
        *[
            pltpu.with_memory_space_constraint(v, pltpu.HBM)
            for v in (
                queries, rows_of(root_kv), rows_of(node_kv), rows_of(own_kv),
                anc_owner, anc_slot, depth_len, seg_len, norm_gain,
            )
        ]
    )


def solution(mesh):
    in_specs = (
        P("branch", None, "blk"),
        P("branch", None, "blk"),
        P("branch", None, None, "blk"),
        P("branch", None, None, "blk"),
        P("branch", None),
        P("branch", None),
        P("branch"),
        P("branch"),
        P("blk"),
    )
    return jax.shard_map(
        on_device, mesh=mesh, in_specs=in_specs, out_specs=P("branch", None, "blk"), check_vma=False
    )
```
